32 devices in a mesh: tm: 8 (over y, x, core), head: 4 (over z).
Axes of the slice: x: 2, y: 2, z: 4, core: 2. Of those that a mesh axis runs over, the one named last changes fastest.
Arguments:
- query: bfloat16 [2048, 4096], P('tm', 'head'), may hold values from -200 to 200
- key_in: bfloat16 [2048, 4096], P('tm', 'head'), may hold values from -7 to 7
- value: bfloat16 [2048, 4096], P('tm', 'head'), may hold values from -6 to 6
- grad_out: bfloat16 [2048, 4096], P('tm', 'head'), may hold values from -6 to 6
- weights: bfloat16 [3, 4096, 4096], P(None, 'tm', 'head'), may hold values from -0.09375 to 0.09375
Outputs:
- grad_input_t: bfloat16 [4096, 2048], P('head', 'tm')
The draws below stay inside these ranges and needn't reach their ends.
All inputs are finite; a program needn't handle non-finite values.
Results may differ from the reference program's by a relative error of at most 0.0091.
Values may be sent and summed in bfloat16 or wider, within the bound.
No kernel may reach another device: no remote copies, remote signals or barrier semaphores. Data moves between devices by JAX's collectives and lax.ppermute only.
A program may use at most 256 MiB of HBM per device.

```python
import jax
import jax.numpy as jnp
from jax import lax

D = 4096
HEADS = 32
HD = 128
PATCHES = 256
FRAMES = 8
TOKENS = 2048


def paired_draw(key):
    base_q = jnp.clip(jax.random.normal(jax.random.fold_in(key, 11), (TOKENS, D), jnp.float32), -6.0, 6.0)
    base_k = jnp.clip(jax.random.normal(jax.random.fold_in(key, 12), (TOKENS, D), jnp.float32), -6.0, 6.0)
    keys = base_k
    queries = base_q
    return (queries, keys)


def draw_query(key, part):
    return paired_draw(key)[0].astype(jnp.bfloat16)


def draw_key_in(key, part):
    return paired_draw(key)[1].astype(jnp.bfloat16)


def levels(stream_key, extent, pieces, least, high):
    def one(axis_at, blocks):
        heights = jax.random.uniform(jax.random.fold_in(jax.random.fold_in(stream_key, 6), axis_at), (blocks,), jnp.float32, least / len(pieces), high / len(pieces))
        return jnp.repeat(jnp.exp(heights), extent[axis_at] // blocks).reshape((-1,) + (1,) * (len(extent) - axis_at - 1))

    level = one(*pieces[0])
    for cut in pieces[1:]:
        level = level * one(*cut)
    return level


def noise(key, extent, spread, limit, shards=(), kind=jnp.bfloat16):
    loudness = levels(key, extent, shards, -0.22, 0.18) if shards else 1.0
    values = jax.random.normal(key, extent, jnp.float32) * spread * loudness
    return jnp.minimum(jnp.maximum(values, -limit), limit).astype(kind)


def setup_inputs(seed: int = 0) -> dict:
    arg_keys = jax.random.split(jax.random.key(seed), 6)
    query = draw_query(jax.random.fold_in(arg_keys[5], 71), 0)
    key_in = draw_key_in(jax.random.fold_in(arg_keys[5], 71), 0)
    value = noise(arg_keys[2], (TOKENS, D), 1.0, 6.0, ((0, 8), (1, 4)))
    grad_out = noise(arg_keys[3], (TOKENS, D), 1.0, 6.0, ((0, 8), (1, 4)))
    weights = noise(arg_keys[4], (3, D, D), D ** -0.5, 0.09375, ((1, 8), (2, 4)))
    return {"query": query, "key_in": key_in, "value": value, "grad_out": grad_out, "weights": weights}


def round_keep(array):
    return lax.optimization_barrier(array.astype(jnp.bfloat16)).astype(jnp.float32)


def reference(query, key_in, value, grad_out, weights):
    scale = 1.0 / (HD ** 0.5)

    def heads(array):
        return array.astype(jnp.float32).reshape(FRAMES, PATCHES, HEADS, HD)

    q_heads = heads(query)
    k_heads = heads(key_in)
    v_heads = heads(value)
    g_heads = heads(grad_out)
    scores = jnp.einsum("fphd,gphd->phfg", q_heads, k_heads) * scale
    probs = jax.nn.softmax(scores, axis=-1)
    probs_b = round_keep(probs)
    attended = jnp.einsum("phfg,gphd->fphd", probs_b, v_heads)
    delta = jnp.transpose(jnp.sum(g_heads * attended, axis=-1), (1, 2, 0))
    grad_probs = jnp.einsum("fphd,gphd->phfg", g_heads, v_heads)
    grad_scores = round_keep(probs * (grad_probs - delta[..., None]))
    grad_value = jnp.einsum("phfg,fphd->gphd", probs_b, g_heads).astype(jnp.bfloat16)
    grad_query = (jnp.einsum("phfg,gphd->fphd", grad_scores, k_heads) * scale).astype(jnp.bfloat16)
    grad_key = (jnp.einsum("phfg,fphd->gphd", grad_scores, q_heads) * scale).astype(jnp.bfloat16)
    grads = [grad_query, grad_key, grad_value]
    total = jnp.zeros((D, TOKENS), jnp.float32)
    for which in range(3):
        flat = grads[which].reshape(TOKENS, D)
        total = total + jnp.dot(weights[which], flat.T, preferred_element_type=jnp.float32)
    return total.astype(jnp.bfloat16)
```

```python
import functools

import jax
import jax.numpy as jnp
from jax import lax
from jax.experimental import pallas as pl
from jax.experimental.pallas import tpu as pltpu
from jax.sharding import PartitionSpec as P

HD = 128
GROUP = 16
CHUNKS = 4

F32 = jnp.float32
BF16 = jnp.bfloat16


def temporal(q_heads, k_heads, v_heads, g_heads):
    scale = 1.0 / q_heads.shape[-1] ** 0.5
    scores = jnp.einsum("fphd,gphd->phfg", q_heads, k_heads, preferred_element_type=F32) * scale
    probs = jax.nn.softmax(scores, axis=-1)
    probs_b = probs.astype(BF16)
    attended = jnp.einsum("phfg,gphd->fphd", probs_b, v_heads, preferred_element_type=F32)
    delta = jnp.transpose(jnp.sum(g_heads.astype(F32) * attended, axis=-1), (1, 2, 0))
    grad_probs = jnp.einsum("fphd,gphd->phfg", g_heads, v_heads, preferred_element_type=F32)
    grad_scores = (probs * (grad_probs - delta[..., None])).astype(BF16)
    grad_value = jnp.einsum("phfg,fphd->gphd", probs_b, g_heads, preferred_element_type=F32)
    grad_query = jnp.einsum("phfg,gphd->fphd", grad_scores, k_heads, preferred_element_type=F32)
    grad_key = jnp.einsum("phfg,fphd->gphd", grad_scores, q_heads, preferred_element_type=F32)
    return (
        (grad_query * scale).astype(BF16),
        (grad_key * scale).astype(BF16),
        grad_value.astype(BF16),
    )


def any_mesh(query, key_in, value, grad_out, weights):
    rows, width = query.shape

    def to_patches(array):
        array = array.reshape(1, rows, width // HD, HD)
        return lax.all_to_all(array, "tm", split_axis=1, concat_axis=0, tiled=True)

    def to_frames(array):
        array = lax.all_to_all(array, "tm", split_axis=0, concat_axis=1, tiled=True)
        return array.reshape(rows, width)

    grads = temporal(*(to_patches(a) for a in (query, key_in, value, grad_out)))
    stacked = jnp.stack([to_frames(g) for g in grads])
    gathered = lax.all_gather(weights, "tm", axis=1, tiled=True)
    partial_sum = jnp.einsum("mic,mtc->it", gathered, stacked, preferred_element_type=F32)
    mine = lax.psum_scatter(partial_sum, "head", scatter_dimension=0, tiled=True)
    return mine.astype(BF16)


def attention_kernel(x0, x1, x2, x3a, x3b, out, *, heads, groups):
    scale = 1.0 / HD**0.5
    rows = 8 * GROUP
    r = lax.broadcasted_iota(jnp.int32, (rows, rows), 0)
    c = lax.broadcasted_iota(jnp.int32, (rows, rows), 1)
    bias = jnp.where((r % GROUP) == (c % GROUP), 0.0, -1e30).astype(F32)
    contract_last = (((1,), (1,)), ((), ()))
    contract_first = (((0,), (0,)), ((), ()))

    for group in range(groups):
        for head in range(heads):
            ps = pl.ds(group * GROUP, GROUP)
            cs = pl.ds(head * HD, HD)

            def load(which):
                last = x3a if which < 2 else x3b
                parts = [x0[which, :, ps, cs], x1[which, :, ps, cs], x2[which, :, ps, cs], last[which % 2, :, ps, cs]]
                return jnp.concatenate(parts, axis=0).reshape(rows, HD)

            q, k, v, g = (load(i) for i in range(4))
            scores = lax.dot_general(k, q, contract_last, preferred_element_type=F32) * scale + bias
            peak = jnp.max(scores, axis=0, keepdims=True)
            e = jnp.exp(scores - peak)
            probs = e * (1.0 / jnp.sum(e, axis=0, keepdims=True))
            probs_b = probs.astype(BF16)
            grad_probs = lax.dot_general(v, g, contract_last, preferred_element_type=F32)
            delta = jnp.sum(probs_b.astype(F32) * grad_probs, axis=0, keepdims=True)
            gs = (probs * (grad_probs - delta)).astype(BF16)
            gq = lax.dot_general(gs, k, contract_first, preferred_element_type=F32) * scale
            gk = jnp.dot(gs, q, preferred_element_type=F32) * scale
            gv = jnp.dot(probs_b, g, preferred_element_type=F32)
            for at, grad in enumerate((gq, gk, gv)):
                out[at, :, ps, cs] = grad.astype(BF16).reshape(8, GROUP, HD)


def attention(x0, x1, x2, x3a, x3b):
    patches, width = x0.shape[2], x0.shape[3]
    per_step = 2
    groups = patches // GROUP

    def spec(n, f):
        return pl.BlockSpec((n, f, patches, per_step * HD), lambda h: (0, 0, 0, h))

    return pl.pallas_call(
        functools.partial(attention_kernel, heads=per_step, groups=groups),
        grid=(width // HD // per_step,),
        in_specs=[spec(4, 2), spec(4, 2), spec(4, 2), spec(2, 2), spec(2, 2)],
        out_specs=spec(3, 8),
        out_shape=jax.ShapeDtypeStruct((3, 8, patches, width), BF16),
        compiler_params=pltpu.CompilerParams(vmem_limit_bytes=48 * 1024 * 1024),
        cost_estimate=pl.CostEstimate(
            flops=10 * 8 * patches * 8 * GROUP * width,
            bytes_accessed=2 * 8 * 7 * patches * width,
            transcendentals=8 * patches * 8 * GROUP * width // HD,
        ),
        name="attention",
    )(x0, x1, x2, x3a, x3b)


def swap(array, bit, n):
    return lax.ppermute(array, "tm", [(i, i ^ bit) for i in range(n)])


def planes(query, key_in, value, grad_out, weights, *, n, m):
    rows, width = query.shape
    half = rows // 2
    core = lax.axis_index("tm") % 2
    pairs = [[i, i + 1] for i in range(0, n, 2)]
    weights = lax.all_gather(weights, "tm", axis=1, tiled=True, axis_index_groups=pairs)

    stacked = jnp.stack([query, key_in, value, grad_out])
    mine = lax.dynamic_slice_in_dim(stacked, core * half, half, 1)
    theirs = lax.dynamic_slice_in_dim(stacked, (1 - core) * half, half, 1)
    pair = jnp.stack([mine, swap(theirs, 1, n)], axis=1)

    size = half // CHUNKS
    def place(bit):
        moves = []
        for t in range(n):
            for z in range(m):
                chip, c = t // 2, t % 2
                moves.append((t * m + z, ((chip ^ z) * 2 + (c ^ bit)) * m + chip))
        return moves

    kept, crossed = [], []
    for at in range(CHUNKS):
        x0 = lax.slice_in_dim(pair, at * size, (at + 1) * size, axis=2)
        x1 = swap(x0, 2, n)
        x2 = swap(x0, 4, n)
        x3a = swap(x1[:2], 4, n)
        x3b = swap(x2[2:], 2, n)
        grads = attention(x0, x1, x2, x3a, x3b).reshape(3, 8 * size, width)
        sums = jnp.einsum("mtj,mij->ti", grads, weights, preferred_element_type=F32).astype(BF16)
        sums = sums.reshape(m, 2, size, sums.shape[-1])
        terms = lax.all_to_all(sums, "head", split_axis=0, concat_axis=0, tiled=True)
        total = jnp.sum(terms.astype(F32), axis=0).astype(BF16)
        kept.append(lax.ppermute(total[0], ("tm", "head"), place(0)))
        crossed.append(lax.ppermute(total[1], ("tm", "head"), place(1)))
    kept = jnp.concatenate(kept, axis=0)
    crossed = jnp.concatenate(crossed, axis=0)
    first = jnp.where(core == 0, kept, crossed)
    second = jnp.where(core == 0, crossed, kept)
    return jnp.concatenate([first, second], axis=0).T


def solution(mesh):
    n, m = mesh.shape["tm"], mesh.shape["head"]
    per_device = functools.partial(planes, n=n, m=m) if n == 8 and m == 4 else any_mesh
    tokens = P("tm", "head")
    return jax.shard_map(
        per_device,
        mesh=mesh,
        in_specs=(tokens, tokens, tokens, tokens, P(None, "tm", "head")),
        out_specs=P("head", "tm"),
        check_vma=False,
    )
```

```python
import functools

import jax
import jax.numpy as jnp
from jax import lax
from jax.experimental import pallas as pl
from jax.experimental.pallas import tpu as pltpu
from jax.sharding import PartitionSpec as P

HD = 128
GROUP = 16
UNITS = 8
VMEM_MIB = 32
TILE = 256
SIZES = (48, 48, 32)

F32 = jnp.float32
BF16 = jnp.bfloat16


def temporal(q_heads, k_heads, v_heads, g_heads):
    scale = 1.0 / q_heads.shape[-1] ** 0.5
    scores = jnp.einsum("fphd,gphd->phfg", q_heads, k_heads, preferred_element_type=F32) * scale
    probs = jax.nn.softmax(scores, axis=-1)
    probs_b = probs.astype(BF16)
    attended = jnp.einsum("phfg,gphd->fphd", probs_b, v_heads, preferred_element_type=F32)
    delta = jnp.transpose(jnp.sum(g_heads.astype(F32) * attended, axis=-1), (1, 2, 0))
    grad_probs = jnp.einsum("fphd,gphd->phfg", g_heads, v_heads, preferred_element_type=F32)
    grad_scores = (probs * (grad_probs - delta[..., None])).astype(BF16)
    grad_value = jnp.einsum("phfg,fphd->gphd", probs_b, g_heads, preferred_element_type=F32)
    grad_query = jnp.einsum("phfg,gphd->fphd", grad_scores, k_heads, preferred_element_type=F32)
    grad_key = jnp.einsum("phfg,fphd->gphd", grad_scores, q_heads, preferred_element_type=F32)
    return (
        (grad_query * scale).astype(BF16),
        (grad_key * scale).astype(BF16),
        grad_value.astype(BF16),
    )


def any_mesh(query, key_in, value, grad_out, weights):
    rows, width = query.shape

    def to_patches(array):
        array = array.reshape(1, rows, width // HD, HD)
        return lax.all_to_all(array, "tm", split_axis=1, concat_axis=0, tiled=True)

    def to_frames(array):
        array = lax.all_to_all(array, "tm", split_axis=0, concat_axis=1, tiled=True)
        return array.reshape(rows, width)

    grads = temporal(*(to_patches(a) for a in (query, key_in, value, grad_out)))
    stacked = jnp.stack([to_frames(g) for g in grads])
    gathered = lax.all_gather(weights, "tm", axis=1, tiled=True)
    partial_sum = jnp.einsum("mic,mtc->it", gathered, stacked, preferred_element_type=F32)
    mine = lax.psum_scatter(partial_sum, "head", scatter_dimension=0, tiled=True)
    return mine.astype(BF16)


def chunk_kernel(info, *refs):
    pieces, (w_own, w_other, keep, pass_on, give, xs, grads, sums, sem) = refs[:5], refs[5:]
    patches, width = pieces[0].shape[2], pieces[0].shape[3]
    features = w_own.shape[1]
    scale = 1.0 / HD**0.5
    log2_scale = scale * 1.4426950408889634
    rows = 8 * GROUP

    per_half = width // 2
    copies = [[], []]
    for half in range(2):
        cs = pl.ds(half * per_half, per_half)
        places = (
            xs.at[:, 0:2, :, cs],
            xs.at[:, 2:4, :, cs],
            xs.at[:, 4:6, :, cs],
            xs.at[0:2, 6:8, :, cs],
            xs.at[2:4, 6:8, :, cs],
        )
        for at, (piece, place) in enumerate(zip(pieces, places)):
            copies[half].append(pltpu.make_async_copy(piece.at[:, :, :, cs], place, sem.at[half, at]))
    for copy in copies[0] + copies[1]:
        copy.start()

    r = lax.broadcasted_iota(jnp.int32, (rows, rows), 0)
    c = lax.broadcasted_iota(jnp.int32, (rows, rows), 1)
    bias = jnp.where((r % GROUP) == (c % GROUP), 0.0, -1e30).astype(F32)
    last = (((1,), (1,)), ((), ()))
    first = (((0,), (0,)), ((), ()))

    def attention(every):
        for start in range(0, len(every), UNITS):
            units = [(pl.ds(g * GROUP, GROUP), pl.ds(h * HD, HD)) for g, h in every[start : start + UNITS]]
            q, k, v, g = ([xs[which, :, ps, cs].reshape(rows, HD) for ps, cs in units] for which in range(4))
            scores = [lax.dot_general(b, a, last, preferred_element_type=F32) + bias for a, b in zip(q, k)]
            grad_probs = [lax.dot_general(b, a, last, preferred_element_type=F32) for a, b in zip(g, v)]
            probs_b, grad_scores = [], []
            for s, gp in zip(scores, grad_probs):
                e = jnp.exp2((s - jnp.max(s, axis=0, keepdims=True)) * log2_scale)
                p = e * (1.0 / jnp.sum(e, axis=0, keepdims=True))
                pb = p.astype(BF16)
                delta = jnp.sum(pb.astype(F32) * gp, axis=0, keepdims=True)
                probs_b.append(pb)
                grad_scores.append((p * (gp - delta)).astype(BF16))
            for at, (ps, cs) in enumerate(units):
                gs, pb = grad_scores[at], probs_b[at]
                gq = lax.dot_general(gs, k[at], first, preferred_element_type=F32) * scale
                gk = jnp.dot(gs, q[at], preferred_element_type=F32) * scale
                gv = jnp.dot(pb, g[at], preferred_element_type=F32)
                for m, grad in enumerate((gq, gk, gv)):
                    grads[m, :, ps, cs] = grad.astype(BF16).reshape(8, GROUP, HD)

    heads = per_half // HD
    for half in range(2):
        for copy in copies[half]:
            copy.wait()
        attention([(g, half * heads + h) for h in range(heads) for g in range(patches // GROUP)])

    for which, ws in enumerate((w_own, w_other)):
        base = (info[4] if which == 0 else 1 - info[4]) * features
        for start in range(0, features, TILE):
            total = None
            for m in range(3):
                flat = grads[m].reshape(8 * patches, width)
                term = lax.dot_general(flat, ws[m, start : start + TILE, :], last, preferred_element_type=F32)
                total = term if total is None else total + term
            sums[:, pl.ds(pl.multiple_of(base + start, TILE), TILE)] = total.astype(BF16)
    part = 2 * patches
    for x in range(4):
        out, row = ((keep, 0), (pass_on, 0), (give, 0), (give, part))[x]
        out[row : row + part, :] = sums[pl.ds(pl.multiple_of(info[x] * part, part), part), :]


def chunk(info, pieces, w_own, w_other):
    patches, width = pieces[0].shape[2], pieces[0].shape[3]
    features = w_own.shape[1]
    vmem = pl.BlockSpec(memory_space=pltpu.VMEM)
    return pl.pallas_call(
        chunk_kernel,
        in_specs=[pl.BlockSpec(memory_space=pltpu.SMEM)] + [pl.BlockSpec(memory_space=pl.ANY)] * 5 + [vmem] * 2,
        out_specs=[vmem] * 3,
        out_shape=[jax.ShapeDtypeStruct((n * patches, 2 * features), BF16) for n in (2, 2, 4)],
        scratch_shapes=[
            pltpu.VMEM((4, 8, patches, width), BF16),
            pltpu.VMEM((3, 8, patches, width), BF16),
            pltpu.VMEM((8 * patches, 2 * features), BF16),
            pltpu.SemaphoreType.DMA((2, 5)),
        ],
        compiler_params=pltpu.CompilerParams(vmem_limit_bytes=VMEM_MIB * 1024 * 1024),
        cost_estimate=pl.CostEstimate(
            flops=96 * patches * width * features + 80 * patches * 8 * GROUP * width,
            bytes_accessed=12 * features * width + 112 * patches * width,
            transcendentals=8 * patches * 8 * GROUP * width // HD,
        ),
        name="attention_and_product",
    )(info, *pieces, w_own, w_other)


def lay_kernel(core, *refs):
    kept, crossed, out = refs[: len(refs) // 2], refs[len(refs) // 2 : -1], refs[-1]
    half = out.shape[1] // 2
    for side, parts in enumerate((kept, crossed)):
        whole = jnp.concatenate([part[...] for part in parts], axis=0)
        at = (core[0] if side == 0 else 1 - core[0]) * half
        out[:, pl.ds(pl.multiple_of(at, half), half)] = whole.T


def lay_out(core, kept, crossed):
    vmem = pl.BlockSpec(memory_space=pltpu.VMEM)
    shape = (kept[0].shape[1], 2 * sum(k.shape[0] for k in kept))
    return pl.pallas_call(
        lay_kernel,
        in_specs=[pl.BlockSpec(memory_space=pltpu.SMEM)] + [vmem] * (2 * len(kept)),
        out_specs=vmem,
        out_shape=jax.ShapeDtypeStruct(shape, BF16),
        name="lay_out",
    )(core, *kept, *crossed)


def swap(array, bit, n):
    return lax.ppermute(array, "tm", [(i, i ^ bit) for i in range(n)])


def after(array, *others):
    return lax.optimization_barrier((array, *others))[0]


COLUMN = ((0, 1, 2, 3), (2, 3, 0, 1), (3, 2, 1, 0), (1, 0, 3, 2))


def planes(query, key_in, value, grad_out, weights, *, n, m):
    rows, width = query.shape
    half = rows // 2
    chip, core = lax.axis_index("tm") // 2, lax.axis_index("tm") % 2
    plane = lax.axis_index("head")
    table = [[[COLUMN[r][z ^ x] ^ r for x in (0, 2, 1, 3)] for z in range(m)] for r in range(n // 2)]
    info = jnp.append(jnp.asarray(table, jnp.int32)[chip, plane], core)

    def half_of(which):
        arrays = (query, key_in, value, grad_out)
        return jnp.stack([lax.dynamic_slice_in_dim(a, which * half, half, 0) for a in arrays])

    theirs = swap(half_of(1 - core), 1, n)
    pair = jnp.stack([half_of(core), theirs], axis=1)
    other = swap(weights, 1, n)

    def move(array, to):
        pairs = [(t * m + z, to(t // 2, t % 2, z)) for t in range(n) for z in range(m)]
        return lax.ppermute(array, ("tm", "head"), pairs)

    def in_plane(array):
        return move(array, lambda r, c, z: (COLUMN[r][z] * 2 + c) * m + z)

    def along_column(array, bit):
        source = {(COLUMN[r][z], z): r for r in range(n // 2) for z in range(m)}
        return move(array, lambda s, c, z: (s * 2 + (c ^ bit)) * m + source[s, z])

    def at_once(array, bit):
        return move(array, lambda r, c, z: (COLUMN[r][z] * 2 + (c ^ bit)) * m + r)

    def give_to(array, bit):
        return lax.ppermute(array, "head", [(z, z ^ bit) for z in range(m)])

    def add(a, b):
        return (a.astype(F32) + b.astype(F32)).astype(BF16)

    def together(*arrays):
        return lax.optimization_barrier(arrays)

    sizes = SIZES
    count = len(sizes)
    own = [lax.slice_in_dim(pair, sum(sizes[:i]), sum(sizes[: i + 1]), axis=2) for i in range(count)]
    kernel, sums, moved = {}, {}, {}
    kept, crossed = [None] * count, [None] * count

    def first_add(k, got):
        keep, pass_on, _ = kernel[k]
        quarter = 2 * sizes[k]
        return add(keep, got[:quarter]), add(pass_on, got[quarter:])

    def final_moves(k):
        size = sizes[k]
        return along_column(moved[k][:size], 0), along_column(moved[k][size:], 1)

    x1, x2 = swap(own[0], 2, n), swap(own[0], 4, n)
    low = high = None
    for k in range(count):
        gate = [kernel[k - 1][0]] if k >= 1 else []
        if k >= 2:
            sums[k - 2] = add(lows, give_to(highs, 2))
            gate += [sums[k - 2]]
        g1, g2 = together(x1, x2, *gate)[:2]
        g1, g2 = g1[:2], g2[2:]
        last = k == count - 1
        if not last:
            following = together(own[k + 1], g1, g2)[0]
            n1, n2 = swap(following, 2, n), swap(following, 4, n)
        pieces = (own[k], x1, x2, swap(g1, 4, n), swap(g2, 2, n))
        gate = []
        if k >= 1:
            lows, highs = first_add(k - 1, got)
            gate += [highs]
        if k >= 2:
            moved[k - 2] = in_plane(sums[k - 2])
            gate += [moved[k - 2]]
        pieces = together(*pieces, *gate)[:5]
        kernel[k] = chunk(info, pieces, weights, other)
        got = give_to(kernel[k][2], 1)
        if not last:
            x1, x2 = n1, n2

    k = count - 1
    got2 = give_to(highs, 2)
    if count >= 3:
        kept[k - 2], crossed[k - 2] = final_moves(k - 2)
        got, got2, kept[k - 2], crossed[k - 2] = together(got, got2, kept[k - 2], crossed[k - 2])
    else:
        got, got2 = together(got, got2)
    sums[k - 1] = add(lows, got2)
    lows, highs = first_add(k, got)
    got2 = give_to(highs, 2)
    moved[k - 1] = in_plane(sums[k - 1])
    got2, moved[k - 1] = together(got2, moved[k - 1])
    sums[k] = add(lows, got2)
    kept[k - 1], crossed[k - 1] = final_moves(k - 1)
    kept[k], crossed[k] = at_once(sums[k][: sizes[k]], 0), at_once(sums[k][sizes[k] :], 1)
    for at in range(count - 3):
        kept[at], crossed[at] = final_moves(at)
    return lay_out(core.reshape(1), kept, crossed)


def solution(mesh):
    n, m = mesh.shape["tm"], mesh.shape["head"]
    per_device = functools.partial(planes, n=n, m=m) if n == 8 and m == 4 else any_mesh
    tokens = P("tm", "head")
    return jax.shard_map(
        per_device,
        mesh=mesh,
        in_specs=(tokens, tokens, tokens, tokens, P(None, "tm", "head")),
        out_specs=P("head", "tm"),
        check_vma=False,
    )
```

```python
import functools

import jax
import jax.numpy as jnp
from jax import lax
from jax.experimental import pallas as pl
from jax.experimental.pallas import tpu as pltpu
from jax.sharding import PartitionSpec as P

HD = 128
GROUP = 16
UNITS = 8
VMEM_MIB = 32
TILE = 256
WEIGHT = 30
SIZES = (48, 48, 32)

F32 = jnp.float32
BF16 = jnp.bfloat16


def temporal(q_heads, k_heads, v_heads, g_heads):
    scale = 1.0 / q_heads.shape[-1] ** 0.5
    scores = jnp.einsum("fphd,gphd->phfg", q_heads, k_heads, preferred_element_type=F32) * scale
    probs = jax.nn.softmax(scores, axis=-1)
    probs_b = probs.astype(BF16)
    attended = jnp.einsum("phfg,gphd->fphd", probs_b, v_heads, preferred_element_type=F32)
    delta = jnp.transpose(jnp.sum(g_heads.astype(F32) * attended, axis=-1), (1, 2, 0))
    grad_probs = jnp.einsum("fphd,gphd->phfg", g_heads, v_heads, preferred_element_type=F32)
    grad_scores = (probs * (grad_probs - delta[..., None])).astype(BF16)
    grad_value = jnp.einsum("phfg,fphd->gphd", probs_b, g_heads, preferred_element_type=F32)
    grad_query = jnp.einsum("phfg,gphd->fphd", grad_scores, k_heads, preferred_element_type=F32)
    grad_key = jnp.einsum("phfg,fphd->gphd", grad_scores, q_heads, preferred_element_type=F32)
    return (
        (grad_query * scale).astype(BF16),
        (grad_key * scale).astype(BF16),
        grad_value.astype(BF16),
    )


def any_mesh(query, key_in, value, grad_out, weights):
    rows, width = query.shape

    def to_patches(array):
        array = array.reshape(1, rows, width // HD, HD)
        return lax.all_to_all(array, "tm", split_axis=1, concat_axis=0, tiled=True)

    def to_frames(array):
        array = lax.all_to_all(array, "tm", split_axis=0, concat_axis=1, tiled=True)
        return array.reshape(rows, width)

    grads = temporal(*(to_patches(a) for a in (query, key_in, value, grad_out)))
    stacked = jnp.stack([to_frames(g) for g in grads])
    gathered = lax.all_gather(weights, "tm", axis=1, tiled=True)
    partial_sum = jnp.einsum("mic,mtc->it", gathered, stacked, preferred_element_type=F32)
    mine = lax.psum_scatter(partial_sum, "head", scatter_dimension=0, tiled=True)
    return mine.astype(BF16)


def chunk_kernel(info, *refs):
    pieces, (w_own, w_other, keep, pass_on, give, xs, grads, sums, sem) = refs[:5], refs[5:]
    patches, width = pieces[0].shape[2], pieces[0].shape[3]
    features = w_own.shape[1]
    scale = 1.0 / HD**0.5
    log2_scale = scale * 1.4426950408889634
    rows = 8 * GROUP

    per_half = width // 2
    copies = [[], []]
    for half in range(2):
        cs = pl.ds(half * per_half, per_half)
        places = (
            xs.at[:, 0:2, :, cs],
            xs.at[:, 2:4, :, cs],
            xs.at[:, 4:6, :, cs],
            xs.at[0:2, 6:8, :, cs],
            xs.at[2:4, 6:8, :, cs],
        )
        for at, (piece, place) in enumerate(zip(pieces, places)):
            copies[half].append(pltpu.make_async_copy(piece.at[:, :, :, cs], place, sem.at[half, at]))
    for copy in copies[0] + copies[1]:
        copy.start()

    r = lax.broadcasted_iota(jnp.int32, (rows, rows), 0)
    c = lax.broadcasted_iota(jnp.int32, (rows, rows), 1)
    bias = jnp.where((r % GROUP) == (c % GROUP), 0.0, -1e30).astype(F32)
    last = (((1,), (1,)), ((), ()))
    first = (((0,), (0,)), ((), ()))

    def attention(every):
        for start in range(0, len(every), UNITS):
            units = [(pl.ds(g * GROUP, GROUP), pl.ds(h * HD, HD)) for g, h in every[start : start + UNITS]]
            q, k, v, g = ([xs[which, :, ps, cs].reshape(rows, HD) for ps, cs in units] for which in range(4))
            scores = [lax.dot_general(b, a, last, preferred_element_type=F32) + bias for a, b in zip(q, k)]
            grad_probs = [lax.dot_general(b, a, last, preferred_element_type=F32) for a, b in zip(g, v)]
            probs_b, grad_scores = [], []
            for s, gp in zip(scores, grad_probs):
                e = jnp.exp2((s - jnp.max(s, axis=0, keepdims=True)) * log2_scale)
                p = e * (1.0 / jnp.sum(e, axis=0, keepdims=True))
                pb = p.astype(BF16)
                delta = jnp.sum(pb.astype(F32) * gp, axis=0, keepdims=True)
                probs_b.append(pb)
                grad_scores.append((p * (gp - delta)).astype(BF16))
            for at, (ps, cs) in enumerate(units):
                gs, pb = grad_scores[at], probs_b[at]
                gq = lax.dot_general(gs, k[at], first, preferred_element_type=F32) * scale
                gk = jnp.dot(gs, q[at], preferred_element_type=F32) * scale
                gv = jnp.dot(pb, g[at], preferred_element_type=F32)
                for m, grad in enumerate((gq, gk, gv)):
                    grads[m, :, ps, cs] = grad.astype(BF16).reshape(8, GROUP, HD)

    heads = per_half // HD
    for half in range(2):
        for copy in copies[half]:
            copy.wait()
        attention([(g, half * heads + h) for h in range(heads) for g in range(patches // GROUP)])

    for which, ws in enumerate((w_own, w_other)):
        base = (info[4] if which == 0 else 1 - info[4]) * features
        for start in range(0, features, TILE):
            total = None
            for m in range(3):
                flat = grads[m].reshape(8 * patches, width)
                term = lax.dot_general(flat, ws[m, start : start + TILE, :], last, preferred_element_type=F32)
                total = term if total is None else total + term
            sums[:, pl.ds(pl.multiple_of(base + start, TILE), TILE)] = total.astype(BF16)
    part = 2 * patches
    for x in range(4):
        out, row = ((keep, 0), (pass_on, 0), (give, 0), (give, part))[x]
        out[row : row + part, :] = sums[pl.ds(pl.multiple_of(info[x] * part, part), part), :]


def chunk(info, pieces, w_own, w_other):
    patches, width = pieces[0].shape[2], pieces[0].shape[3]
    features = w_own.shape[1]
    vmem = pl.BlockSpec(memory_space=pltpu.VMEM)
    return pl.pallas_call(
        chunk_kernel,
        in_specs=[pl.BlockSpec(memory_space=pltpu.SMEM)] + [pl.BlockSpec(memory_space=pl.ANY)] * 5 + [vmem] * 2,
        out_specs=[vmem] * 3,
        out_shape=[jax.ShapeDtypeStruct((n * patches, 2 * features), BF16) for n in (2, 2, 4)],
        scratch_shapes=[
            pltpu.VMEM((4, 8, patches, width), BF16),
            pltpu.VMEM((3, 8, patches, width), BF16),
            pltpu.VMEM((8 * patches, 2 * features), BF16),
            pltpu.SemaphoreType.DMA((2, 5)),
        ],
        compiler_params=pltpu.CompilerParams(vmem_limit_bytes=VMEM_MIB * 1024 * 1024),
        cost_estimate=pl.CostEstimate(
            flops=WEIGHT * (96 * patches * width * features + 80 * patches * 8 * GROUP * width),
            bytes_accessed=WEIGHT * (12 * features * width + 112 * patches * width),
            transcendentals=WEIGHT * (8 * patches * 8 * GROUP * width // HD),
        ),
        name="attention_and_product",
    )(info, *pieces, w_own, w_other)


def lay_kernel(core, *refs):
    kept, crossed, out = refs[: len(refs) // 2], refs[len(refs) // 2 : -1], refs[-1]
    half = out.shape[1] // 2
    for side, parts in enumerate((kept, crossed)):
        whole = jnp.concatenate([part[...] for part in parts], axis=0)
        at = (core[0] if side == 0 else 1 - core[0]) * half
        out[:, pl.ds(pl.multiple_of(at, half), half)] = whole.T


def lay_out(core, kept, crossed):
    vmem = pl.BlockSpec(memory_space=pltpu.VMEM)
    shape = (kept[0].shape[1], 2 * sum(k.shape[0] for k in kept))
    return pl.pallas_call(
        lay_kernel,
        in_specs=[pl.BlockSpec(memory_space=pltpu.SMEM)] + [vmem] * (2 * len(kept)),
        out_specs=vmem,
        out_shape=jax.ShapeDtypeStruct(shape, BF16),
        name="lay_out",
    )(core, *kept, *crossed)


def swap(array, bit, n):
    return lax.ppermute(array, "tm", [(i, i ^ bit) for i in range(n)])


def after(array, *others):
    return lax.optimization_barrier((array, *others))[0]


COLUMN = ((0, 1, 2, 3), (2, 3, 0, 1), (3, 2, 1, 0), (1, 0, 3, 2))


def planes(query, key_in, value, grad_out, weights, *, n, m):
    rows, width = query.shape
    half = rows // 2
    chip, core = lax.axis_index("tm") // 2, lax.axis_index("tm") % 2
    plane = lax.axis_index("head")
    table = [[[COLUMN[r][z ^ x] ^ r for x in (0, 2, 1, 3)] for z in range(m)] for r in range(n // 2)]
    info = jnp.append(jnp.asarray(table, jnp.int32)[chip, plane], core)

    def half_of(which):
        arrays = (query, key_in, value, grad_out)
        return jnp.stack([lax.dynamic_slice_in_dim(a, which * half, half, 0) for a in arrays])

    theirs = swap(half_of(1 - core), 1, n)
    pair = jnp.stack([half_of(core), theirs], axis=1)
    other = swap(after(weights, theirs), 1, n)

    def move(array, to):
        pairs = [(t * m + z, to(t // 2, t % 2, z)) for t in range(n) for z in range(m)]
        return lax.ppermute(array, ("tm", "head"), pairs)

    def in_plane(array):
        return move(array, lambda r, c, z: (COLUMN[r][z] * 2 + c) * m + z)

    def along_column(array, bit):
        source = {(COLUMN[r][z], z): r for r in range(n // 2) for z in range(m)}
        return move(array, lambda s, c, z: (s * 2 + (c ^ bit)) * m + source[s, z])

    def at_once(array, bit):
        return move(array, lambda r, c, z: (COLUMN[r][z] * 2 + (c ^ bit)) * m + r)

    def give_to(array, bit):
        return lax.ppermute(array, "head", [(z, z ^ bit) for z in range(m)])

    def add(a, b):
        return (a.astype(F32) + b.astype(F32)).astype(BF16)

    def together(*arrays):
        return lax.optimization_barrier(arrays)

    sizes = SIZES
    count = len(sizes)
    own = [lax.slice_in_dim(pair, sum(sizes[:i]), sum(sizes[: i + 1]), axis=2) for i in range(count)]
    kernel, sums, moved = {}, {}, {}
    kept, crossed = [None] * count, [None] * count

    def first_add(k, got):
        keep, pass_on, _ = kernel[k]
        quarter = 2 * sizes[k]
        return add(keep, got[:quarter]), add(pass_on, got[quarter:])

    def final_moves(k):
        size = sizes[k]
        return along_column(moved[k][:size], 0), along_column(moved[k][size:], 1)

    x1, x2 = swap(own[0], 2, n), swap(own[0], 4, n)
    low = high = None
    for k in range(count):
        gate = [kernel[k - 1][0]] if k >= 1 else []
        if k >= 2:
            sums[k - 2] = add(lows, give_to(highs, 2))
            gate += [sums[k - 2]]
        g1, g2 = together(x1, x2, *gate)[:2]
        g1, g2 = g1[:2], g2[2:]
        last = k == count - 1
        if not last:
            following = together(own[k + 1], g1, g2)[0]
            n1, n2 = swap(following, 2, n), swap(following, 4, n)
        pieces = (own[k], x1, x2, swap(g1, 4, n), swap(g2, 2, n))
        gate = []
        if k >= 1:
            lows, highs = first_add(k - 1, got)
            gate += [highs]
        if k >= 2:
            moved[k - 2] = in_plane(sums[k - 2])
            gate += [moved[k - 2]]
        pieces = together(*pieces, *gate)[:5]
        kernel[k] = chunk(info, pieces, weights, other)
        got = give_to(kernel[k][2], 1)
        if not last:
            x1, x2 = n1, n2

    k = count - 1
    got2 = give_to(highs, 2)
    if count >= 3:
        kept[k - 2], crossed[k - 2] = final_moves(k - 2)
        got, got2, kept[k - 2], crossed[k - 2] = together(got, got2, kept[k - 2], crossed[k - 2])
    else:
        got, got2 = together(got, got2)
    sums[k - 1] = add(lows, got2)
    lows, highs = first_add(k, got)
    got2 = give_to(highs, 2)
    moved[k - 1] = in_plane(sums[k - 1])
    got2, moved[k - 1] = together(got2, moved[k - 1])
    sums[k] = add(lows, got2)
    kept[k - 1], crossed[k - 1] = final_moves(k - 1)
    kept[k], crossed[k] = at_once(sums[k][: sizes[k]], 0), at_once(sums[k][sizes[k] :], 1)
    for at in range(count - 3):
        kept[at], crossed[at] = final_moves(at)
    return lay_out(core.reshape(1), kept, crossed)


def solution(mesh):
    n, m = mesh.shape["tm"], mesh.shape["head"]
    per_device = functools.partial(planes, n=n, m=m) if n == 8 and m == 4 else any_mesh
    tokens = P("tm", "head")
    return jax.shard_map(
        per_device,
        mesh=mesh,
        in_specs=(tokens, tokens, tokens, tokens, P(None, "tm", "head")),
        out_specs=P("head", "tm"),
        check_vma=False,
    )
```

```python
import functools

import jax
import jax.numpy as jnp
from jax import lax
from jax.experimental import pallas as pl
from jax.experimental.pallas import tpu as pltpu
from jax.sharding import PartitionSpec as P

HD = 128
GROUP = 16
UNITS = 8
VMEM_MIB = 32
TILE = 256
WEIGHT = 30
SIZES = (48, 48, 32)

F32 = jnp.float32
BF16 = jnp.bfloat16


def temporal(q_heads, k_heads, v_heads, g_heads):
    scale = 1.0 / q_heads.shape[-1] ** 0.5
    scores = jnp.einsum("fphd,gphd->phfg", q_heads, k_heads, preferred_element_type=F32) * scale
    probs = jax.nn.softmax(scores, axis=-1)
    probs_b = probs.astype(BF16)
    attended = jnp.einsum("phfg,gphd->fphd", probs_b, v_heads, preferred_element_type=F32)
    delta = jnp.transpose(jnp.sum(g_heads.astype(F32) * attended, axis=-1), (1, 2, 0))
    grad_probs = jnp.einsum("fphd,gphd->phfg", g_heads, v_heads, preferred_element_type=F32)
    grad_scores = (probs * (grad_probs - delta[..., None])).astype(BF16)
    grad_value = jnp.einsum("phfg,fphd->gphd", probs_b, g_heads, preferred_element_type=F32)
    grad_query = jnp.einsum("phfg,gphd->fphd", grad_scores, k_heads, preferred_element_type=F32)
    grad_key = jnp.einsum("phfg,fphd->gphd", grad_scores, q_heads, preferred_element_type=F32)
    return (
        (grad_query * scale).astype(BF16),
        (grad_key * scale).astype(BF16),
        grad_value.astype(BF16),
    )


def any_mesh(query, key_in, value, grad_out, weights):
    rows, width = query.shape

    def to_patches(array):
        array = array.reshape(1, rows, width // HD, HD)
        return lax.all_to_all(array, "tm", split_axis=1, concat_axis=0, tiled=True)

    def to_frames(array):
        array = lax.all_to_all(array, "tm", split_axis=0, concat_axis=1, tiled=True)
        return array.reshape(rows, width)

    grads = temporal(*(to_patches(a) for a in (query, key_in, value, grad_out)))
    stacked = jnp.stack([to_frames(g) for g in grads])
    gathered = lax.all_gather(weights, "tm", axis=1, tiled=True)
    partial_sum = jnp.einsum("mic,mtc->it", gathered, stacked, preferred_element_type=F32)
    mine = lax.psum_scatter(partial_sum, "head", scatter_dimension=0, tiled=True)
    return mine.astype(BF16)


def chunk_kernel(info, *refs):
    pieces, (w_own, w_other, keep, pass_on, give, xs, grads, sums, sem) = refs[:5], refs[5:]
    patches, width = pieces[0].shape[2], pieces[0].shape[3]
    features = w_own.shape[1]
    scale = 1.0 / HD**0.5
    log2_scale = scale * 1.4426950408889634
    rows = 8 * GROUP

    per_half = width // 2
    copies = [[], []]
    for half in range(2):
        cs = pl.ds(half * per_half, per_half)
        places = (
            xs.at[:, 0:2, :, cs],
            xs.at[:, 2:4, :, cs],
            xs.at[:, 4:6, :, cs],
            xs.at[0:2, 6:8, :, cs],
            xs.at[2:4, 6:8, :, cs],
        )
        for at, (piece, place) in enumerate(zip(pieces, places)):
            copies[half].append(pltpu.make_async_copy(piece.at[:, :, :, cs], place, sem.at[half, at]))
    for copy in copies[0] + copies[1]:
        copy.start()

    r = lax.broadcasted_iota(jnp.int32, (rows, rows), 0)
    c = lax.broadcasted_iota(jnp.int32, (rows, rows), 1)
    bias = jnp.where((r % GROUP) == (c % GROUP), 0.0, -1e30).astype(F32)
    last = (((1,), (1,)), ((), ()))
    first = (((0,), (0,)), ((), ()))

    def attention(every):
        for start in range(0, len(every), UNITS):
            units = [(pl.ds(g * GROUP, GROUP), pl.ds(h * HD, HD)) for g, h in every[start : start + UNITS]]
            q, k, v, g = ([xs[which, :, ps, cs].reshape(rows, HD) for ps, cs in units] for which in range(4))
            scores = [lax.dot_general(b, a, last, preferred_element_type=F32) + bias for a, b in zip(q, k)]
            grad_probs = [lax.dot_general(b, a, last, preferred_element_type=F32) for a, b in zip(g, v)]
            probs_b, grad_scores = [], []
            for s, gp in zip(scores, grad_probs):
                e = jnp.exp2((s - jnp.max(s, axis=0, keepdims=True)) * log2_scale)
                p = e * (1.0 / jnp.sum(e, axis=0, keepdims=True))
                pb = p.astype(BF16)
                delta = jnp.sum(pb.astype(F32) * gp, axis=0, keepdims=True)
                probs_b.append(pb)
                grad_scores.append((p * (gp - delta)).astype(BF16))
            for at, (ps, cs) in enumerate(units):
                gs, pb = grad_scores[at], probs_b[at]
                gq = lax.dot_general(gs, k[at], first, preferred_element_type=F32) * scale
                gk = jnp.dot(gs, q[at], preferred_element_type=F32) * scale
                gv = jnp.dot(pb, g[at], preferred_element_type=F32)
                for m, grad in enumerate((gq, gk, gv)):
                    grads[m, :, ps, cs] = grad.astype(BF16).reshape(8, GROUP, HD)

    heads = per_half // HD
    for half in range(2):
        for copy in copies[half]:
            copy.wait()
        attention([(g, half * heads + h) for h in range(heads) for g in range(patches // GROUP)])

    for which, ws in enumerate((w_own, w_other)):
        base = (info[4] if which == 0 else 1 - info[4]) * features
        for start in range(0, features, TILE):
            total = None
            for m in range(3):
                flat = grads[m].reshape(8 * patches, width)
                term = lax.dot_general(flat, ws[m, start : start + TILE, :], last, preferred_element_type=F32)
                total = term if total is None else total + term
            sums[:, pl.ds(pl.multiple_of(base + start, TILE), TILE)] = total.astype(BF16)
    part = 2 * patches
    for x in range(4):
        out, row = ((keep, 0), (pass_on, 0), (give, 0), (give, part))[x]
        out[row : row + part, :] = sums[pl.ds(pl.multiple_of(info[x] * part, part), part), :]


def chunk(info, pieces, w_own, w_other):
    patches, width = pieces[0].shape[2], pieces[0].shape[3]
    features = w_own.shape[1]
    vmem = pl.BlockSpec(memory_space=pltpu.VMEM)
    return pl.pallas_call(
        chunk_kernel,
        in_specs=[pl.BlockSpec(memory_space=pltpu.SMEM)] + [pl.BlockSpec(memory_space=pl.ANY)] * 5 + [vmem] * 2,
        out_specs=[vmem] * 3,
        out_shape=[jax.ShapeDtypeStruct((n * patches, 2 * features), BF16) for n in (2, 2, 4)],
        scratch_shapes=[
            pltpu.VMEM((4, 8, patches, width), BF16),
            pltpu.VMEM((3, 8, patches, width), BF16),
            pltpu.VMEM((8 * patches, 2 * features), BF16),
            pltpu.SemaphoreType.DMA((2, 5)),
        ],
        compiler_params=pltpu.CompilerParams(vmem_limit_bytes=VMEM_MIB * 1024 * 1024),
        cost_estimate=pl.CostEstimate(
            flops=WEIGHT * (96 * patches * width * features + 80 * patches * 8 * GROUP * width),
            bytes_accessed=WEIGHT * (12 * features * width + 112 * patches * width),
            transcendentals=WEIGHT * (8 * patches * 8 * GROUP * width // HD),
        ),
        name="attention_and_product",
    )(info, *pieces, w_own, w_other)


def lay_kernel(core, *refs):
    kept, crossed, out = refs[:-2], refs[-2:-1], refs[-1]
    half = out.shape[1] // 2
    for side, parts in enumerate((kept, crossed)):
        whole = jnp.concatenate([part[...] for part in parts], axis=0)
        at = (core[0] if side == 0 else 1 - core[0]) * half
        out[:, pl.ds(pl.multiple_of(at, half), half)] = whole.T


def lay_out(core, kept, crossed):
    vmem = pl.BlockSpec(memory_space=pltpu.VMEM)
    shape = (kept[0].shape[1], 2 * crossed[0].shape[0])
    return pl.pallas_call(
        lay_kernel,
        in_specs=[pl.BlockSpec(memory_space=pltpu.SMEM)] + [vmem] * (len(kept) + 1),
        out_specs=vmem,
        out_shape=jax.ShapeDtypeStruct(shape, BF16),
        name="lay_out",
    )(core, *kept, *crossed)


def swap(array, bit, n):
    return lax.ppermute(array, "tm", [(i, i ^ bit) for i in range(n)])


def after(array, *others):
    return lax.optimization_barrier((array, *others))[0]


COLUMN = ((0, 1, 2, 3), (2, 3, 0, 1), (3, 2, 1, 0), (1, 0, 3, 2))


def planes(query, key_in, value, grad_out, weights, *, n, m):
    rows, width = query.shape
    half = rows // 2
    chip, core = lax.axis_index("tm") // 2, lax.axis_index("tm") % 2
    plane = lax.axis_index("head")
    table = [[[COLUMN[r][z ^ x] ^ r for x in (0, 2, 1, 3)] for z in range(m)] for r in range(n // 2)]
    info = jnp.append(jnp.asarray(table, jnp.int32)[chip, plane], core)

    def half_of(which):
        arrays = (query, key_in, value, grad_out)
        return jnp.stack([lax.dynamic_slice_in_dim(a, which * half, half, 0) for a in arrays])

    theirs = swap(half_of(1 - core), 1, n)
    pair = jnp.stack([half_of(core), theirs], axis=1)
    other = swap(after(weights, theirs), 1, n)

    def move(array, to):
        pairs = [(t * m + z, to(t // 2, t % 2, z)) for t in range(n) for z in range(m)]
        return lax.ppermute(array, ("tm", "head"), pairs)

    def in_plane(array):
        return move(array, lambda r, c, z: (COLUMN[r][z] * 2 + c) * m + z)

    def along_column(array):
        source = {(COLUMN[r][z], z): r for r in range(n // 2) for z in range(m)}
        return move(array, lambda s, c, z: (s * 2 + c) * m + source[s, z])

    def at_once(array, bit):
        return move(array, lambda r, c, z: (COLUMN[r][z] * 2 + (c ^ bit)) * m + r)

    def give_to(array, bit):
        return lax.ppermute(array, "head", [(z, z ^ bit) for z in range(m)])

    def add(a, b):
        return (a.astype(F32) + b.astype(F32)).astype(BF16)

    def together(*arrays):
        return lax.optimization_barrier(arrays)

    sizes = SIZES
    count = len(sizes)
    own = [lax.slice_in_dim(pair, sum(sizes[:i]), sum(sizes[: i + 1]), axis=2) for i in range(count)]
    kernel, sums, moved = {}, {}, {}

    def first_add(k, got):
        keep, pass_on, _ = kernel[k]
        quarter = 2 * sizes[k]
        return add(keep, got[:quarter]), add(pass_on, got[quarter:])

    x1, x2 = swap(own[0], 2, n), swap(own[0], 4, n)
    low = high = None
    for k in range(count):
        gate = [kernel[k - 1][0]] if k >= 1 else []
        if k >= 2:
            sums[k - 2] = add(lows, give_to(highs, 2))
            gate += [sums[k - 2]]
        g1, g2 = together(x1, x2, *gate)[:2]
        g1, g2 = g1[:2], g2[2:]
        last = k == count - 1
        if not last:
            following = together(own[k + 1], g1, g2)[0]
            n1, n2 = swap(following, 2, n), swap(following, 4, n)
        pieces = (own[k], x1, x2, swap(g1, 4, n), swap(g2, 2, n))
        gate = []
        if k >= 1 and not last:
            lows, highs = first_add(k - 1, got)
            gate += [highs]
        if k >= 2:
            moved[k - 2] = in_plane(sums[k - 2])
            gate += [moved[k - 2]]
        pieces = together(*pieces, *gate)[:5]
        kernel[k] = chunk(info, pieces, weights, other)
        if last:
            lows, highs = first_add(k - 1, together(got, kernel[k][0])[0])
        got = give_to(kernel[k][2], 1)
        if not last:
            x1, x2 = n1, n2

    k = count - 1
    got2 = give_to(highs, 2)
    low, high = first_add(k, together(got, highs)[0])
    sums[k - 1] = add(lows, together(got2, high)[0])
    moved[k - 1] = in_plane(sums[k - 1])
    sums[k] = add(low, give_to(high, 2))
    early = jnp.concatenate([moved[at].reshape(2, sizes[at], -1) for at in range(k)], axis=1)
    early, final = together(along_column(together(early, sums[k])[0]), at_once(sums[k], 0))
    kept = [early[0], final[: sizes[k]]]
    crossed = [swap(jnp.concatenate([early[1], final[sizes[k] :]], axis=0), 1, n)]
    return lay_out(core.reshape(1), kept, crossed)


def solution(mesh):
    n, m = mesh.shape["tm"], mesh.shape["head"]
    per_device = functools.partial(planes, n=n, m=m) if n == 8 and m == 4 else any_mesh
    tokens = P("tm", "head")
    return jax.shard_map(
        per_device,
        mesh=mesh,
        in_specs=(tokens, tokens, tokens, tokens, P(None, "tm", "head")),
        out_specs=P("head", "tm"),
        check_vma=False,
    )
```

```python
import functools

import jax
import jax.numpy as jnp
from jax import lax
from jax.experimental import pallas as pl
from jax.experimental.pallas import tpu as pltpu
from jax.sharding import PartitionSpec as P

HD = 128
GROUP = 16
UNITS = 12
VMEM_MIB = 32
TILE = 256
WEIGHT = 30
SIZES = (48, 48, 32)

F32 = jnp.float32
BF16 = jnp.bfloat16


def temporal(q_heads, k_heads, v_heads, g_heads):
    scale = 1.0 / q_heads.shape[-1] ** 0.5
    scores = jnp.einsum("fphd,gphd->phfg", q_heads, k_heads, preferred_element_type=F32) * scale
    probs = jax.nn.softmax(scores, axis=-1)
    probs_b = probs.astype(BF16)
    attended = jnp.einsum("phfg,gphd->fphd", probs_b, v_heads, preferred_element_type=F32)
    delta = jnp.transpose(jnp.sum(g_heads.astype(F32) * attended, axis=-1), (1, 2, 0))
    grad_probs = jnp.einsum("fphd,gphd->phfg", g_heads, v_heads, preferred_element_type=F32)
    grad_scores = (probs * (grad_probs - delta[..., None])).astype(BF16)
    grad_value = jnp.einsum("phfg,fphd->gphd", probs_b, g_heads, preferred_element_type=F32)
    grad_query = jnp.einsum("phfg,gphd->fphd", grad_scores, k_heads, preferred_element_type=F32)
    grad_key = jnp.einsum("phfg,fphd->gphd", grad_scores, q_heads, preferred_element_type=F32)
    return (
        (grad_query * scale).astype(BF16),
        (grad_key * scale).astype(BF16),
        grad_value.astype(BF16),
    )


def any_mesh(query, key_in, value, grad_out, weights):
    rows, width = query.shape

    def to_patches(array):
        array = array.reshape(1, rows, width // HD, HD)
        return lax.all_to_all(array, "tm", split_axis=1, concat_axis=0, tiled=True)

    def to_frames(array):
        array = lax.all_to_all(array, "tm", split_axis=0, concat_axis=1, tiled=True)
        return array.reshape(rows, width)

    grads = temporal(*(to_patches(a) for a in (query, key_in, value, grad_out)))
    stacked = jnp.stack([to_frames(g) for g in grads])
    gathered = lax.all_gather(weights, "tm", axis=1, tiled=True)
    partial_sum = jnp.einsum("mic,mtc->it", gathered, stacked, preferred_element_type=F32)
    mine = lax.psum_scatter(partial_sum, "head", scatter_dimension=0, tiled=True)
    return mine.astype(BF16)


def chunk_kernel(info, *refs):
    pieces, (w_own, w_other, keep, pass_on, give, xs, grads, sums, sem) = refs[:5], refs[5:]
    patches, width = pieces[0].shape[2], pieces[0].shape[3]
    features = w_own.shape[1]
    scale = 1.0 / HD**0.5
    log2_scale = scale * 1.4426950408889634
    rows = 8 * GROUP

    per_half = width // 2
    copies = [[], []]
    for half in range(2):
        cs = pl.ds(half * per_half, per_half)
        places = (
            xs.at[:, 0:2, :, cs],
            xs.at[:, 2:4, :, cs],
            xs.at[:, 4:6, :, cs],
            xs.at[0:2, 6:8, :, cs],
            xs.at[2:4, 6:8, :, cs],
        )
        for at, (piece, place) in enumerate(zip(pieces, places)):
            copies[half].append(pltpu.make_async_copy(piece.at[:, :, :, cs], place, sem.at[half, at]))
    for copy in copies[0] + copies[1]:
        copy.start()

    r = lax.broadcasted_iota(jnp.int32, (rows, rows), 0)
    c = lax.broadcasted_iota(jnp.int32, (rows, rows), 1)
    bias = jnp.where((r % GROUP) == (c % GROUP), 0.0, -1e30).astype(F32)
    last = (((1,), (1,)), ((), ()))
    first = (((0,), (0,)), ((), ()))

    def attention(every):
        for start in range(0, len(every), UNITS):
            units = [(pl.ds(g * GROUP, GROUP), pl.ds(h * HD, HD)) for g, h in every[start : start + UNITS]]
            q, k, v, g = ([xs[which, :, ps, cs].reshape(rows, HD) for ps, cs in units] for which in range(4))
            scores = [lax.dot_general(b, a, last, preferred_element_type=F32) + bias for a, b in zip(q, k)]
            grad_probs = [lax.dot_general(b, a, last, preferred_element_type=F32) for a, b in zip(g, v)]
            probs_b, grad_scores = [], []
            for s, gp in zip(scores, grad_probs):
                e = jnp.exp2((s - jnp.max(s, axis=0, keepdims=True)) * log2_scale)
                p = e * (1.0 / jnp.sum(e, axis=0, keepdims=True))
                pb = p.astype(BF16)
                delta = jnp.sum(pb.astype(F32) * gp, axis=0, keepdims=True)
                probs_b.append(pb)
                grad_scores.append((p * (gp - delta)).astype(BF16))
            for at, (ps, cs) in enumerate(units):
                gs, pb = grad_scores[at], probs_b[at]
                gq = lax.dot_general(gs, k[at], first, preferred_element_type=F32) * scale
                gk = jnp.dot(gs, q[at], preferred_element_type=F32) * scale
                gv = jnp.dot(pb, g[at], preferred_element_type=F32)
                for m, grad in enumerate((gq, gk, gv)):
                    grads[m, :, ps, cs] = grad.astype(BF16).reshape(8, GROUP, HD)

    heads = per_half // HD
    for half in range(2):
        for copy in copies[half]:
            copy.wait()
        attention([(g, half * heads + h) for h in range(heads) for g in range(patches // GROUP)])

    for which, ws in enumerate((w_own, w_other)):
        base = (info[4] if which == 0 else 1 - info[4]) * features
        for start in range(0, features, TILE):
            total = None
            for m in range(3):
                flat = grads[m].reshape(8 * patches, width)
                term = lax.dot_general(flat, ws[m, start : start + TILE, :], last, preferred_element_type=F32)
                total = term if total is None else total + term
            sums[:, pl.ds(pl.multiple_of(base + start, TILE), TILE)] = total.astype(BF16)
    part = 2 * patches
    for x in range(4):
        out, row = ((keep, 0), (pass_on, 0), (give, 0), (give, part))[x]
        out[row : row + part, :] = sums[pl.ds(pl.multiple_of(info[x] * part, part), part), :]


def chunk(info, pieces, w_own, w_other):
    patches, width = pieces[0].shape[2], pieces[0].shape[3]
    features = w_own.shape[1]
    vmem = pl.BlockSpec(memory_space=pltpu.VMEM)
    return pl.pallas_call(
        chunk_kernel,
        in_specs=[pl.BlockSpec(memory_space=pltpu.SMEM)] + [pl.BlockSpec(memory_space=pl.ANY)] * 5 + [vmem] * 2,
        out_specs=[vmem] * 3,
        out_shape=[jax.ShapeDtypeStruct((n * patches, 2 * features), BF16) for n in (2, 2, 4)],
        scratch_shapes=[
            pltpu.VMEM((4, 8, patches, width), BF16),
            pltpu.VMEM((3, 8, patches, width), BF16),
            pltpu.VMEM((8 * patches, 2 * features), BF16),
            pltpu.SemaphoreType.DMA((2, 5)),
        ],
        compiler_params=pltpu.CompilerParams(vmem_limit_bytes=VMEM_MIB * 1024 * 1024),
        cost_estimate=pl.CostEstimate(
            flops=WEIGHT * (96 * patches * width * features + 80 * patches * 8 * GROUP * width),
            bytes_accessed=WEIGHT * (12 * features * width + 112 * patches * width),
            transcendentals=WEIGHT * (8 * patches * 8 * GROUP * width // HD),
        ),
        name="attention_and_product",
    )(info, *pieces, w_own, w_other)


def lay_kernel(core, early, final, crossed, out, kept_buffer, crossed_buffer, sem):
    half, size = crossed.shape[0], early.shape[1]
    copies = [
        pltpu.make_async_copy(early.at[0], kept_buffer.at[0:size], sem.at[0]),
        pltpu.make_async_copy(final.at[0 : half - size], kept_buffer.at[size:half], sem.at[1]),
        pltpu.make_async_copy(crossed, crossed_buffer, sem.at[2]),
    ]
    for copy in copies:
        copy.start()
    copies[0].wait()
    copies[1].wait()
    out[:, pl.ds(pl.multiple_of(core[0] * half, half), half)] = kept_buffer[...].T
    copies[2].wait()
    out[:, pl.ds(pl.multiple_of((1 - core[0]) * half, half), half)] = crossed_buffer[...].T


def lay_out(core, early, final, crossed):
    half, features = crossed.shape
    return pl.pallas_call(
        lay_kernel,
        in_specs=[pl.BlockSpec(memory_space=pltpu.SMEM)] + [pl.BlockSpec(memory_space=pl.ANY)] * 3,
        out_specs=pl.BlockSpec(memory_space=pltpu.VMEM),
        out_shape=jax.ShapeDtypeStruct((features, 2 * half), BF16),
        scratch_shapes=[
            pltpu.VMEM((half, features), BF16),
            pltpu.VMEM((half, features), BF16),
            pltpu.SemaphoreType.DMA((3,)),
        ],
        name="lay_out",
    )(core, early, final, crossed)


def swap(array, bit, n):
    return lax.ppermute(array, "tm", [(i, i ^ bit) for i in range(n)])


def after(array, *others):
    return lax.optimization_barrier((array, *others))[0]


COLUMN = ((0, 1, 2, 3), (2, 3, 0, 1), (3, 2, 1, 0), (1, 0, 3, 2))


def planes(query, key_in, value, grad_out, weights, *, n, m):
    rows, width = query.shape
    half = rows // 2
    chip, core = lax.axis_index("tm") // 2, lax.axis_index("tm") % 2
    plane = lax.axis_index("head")
    table = [[[COLUMN[r][z ^ x] ^ r for x in (0, 2, 1, 3)] for z in range(m)] for r in range(n // 2)]
    info = jnp.append(jnp.asarray(table, jnp.int32)[chip, plane], core)

    def half_of(which):
        arrays = (query, key_in, value, grad_out)
        return jnp.stack([lax.dynamic_slice_in_dim(a, which * half, half, 0) for a in arrays])

    theirs = swap(half_of(1 - core), 1, n)
    pair = jnp.stack([half_of(core), theirs], axis=1)
    other = swap(after(weights, theirs), 1, n)

    def move(array, to):
        pairs = [(t * m + z, to(t // 2, t % 2, z)) for t in range(n) for z in range(m)]
        return lax.ppermute(array, ("tm", "head"), pairs)

    def in_plane(array):
        return move(array, lambda r, c, z: (COLUMN[r][z] * 2 + c) * m + z)

    def along_column(array):
        source = {(COLUMN[r][z], z): r for r in range(n // 2) for z in range(m)}
        return move(array, lambda s, c, z: (s * 2 + c) * m + source[s, z])

    def at_once(array, bit):
        return move(array, lambda r, c, z: (COLUMN[r][z] * 2 + (c ^ bit)) * m + r)

    def give_to(array, bit):
        return lax.ppermute(array, "head", [(z, z ^ bit) for z in range(m)])

    def add(a, b):
        return (a.astype(F32) + b.astype(F32)).astype(BF16)

    def together(*arrays):
        return lax.optimization_barrier(arrays)

    sizes = SIZES
    count = len(sizes)
    own = [lax.slice_in_dim(pair, sum(sizes[:i]), sum(sizes[: i + 1]), axis=2) for i in range(count)]
    kernel, sums, moved = {}, {}, {}

    def first_add(k, got):
        keep, pass_on, _ = kernel[k]
        quarter = 2 * sizes[k]
        return add(keep, got[:quarter]), add(pass_on, got[quarter:])

    x1, x2 = swap(own[0], 2, n), swap(own[0], 4, n)
    low = high = None
    for k in range(count):
        gate = [kernel[k - 1][0]] if k >= 1 else []
        if k >= 2:
            sums[k - 2] = add(lows, give_to(highs, 2))
            gate += [sums[k - 2]]
        g1, g2 = together(x1, x2, *gate)[:2]
        g1, g2 = g1[:2], g2[2:]
        last = k == count - 1
        if not last:
            following = together(own[k + 1], g1, g2)[0]
            n1, n2 = swap(following, 2, n), swap(following, 4, n)
        pieces = (own[k], x1, x2, swap(g1, 4, n), swap(g2, 2, n))
        gate = []
        if k >= 1 and not last:
            lows, highs = first_add(k - 1, got)
            gate += [highs]
        pieces = together(*pieces, *gate)[:5]
        kernel[k] = chunk(info, pieces, weights, other)
        if last:
            lows, highs = first_add(k - 1, together(got, kernel[k][0])[0])
        got = give_to(kernel[k][2], 1)
        if not last:
            x1, x2 = n1, n2

    k = count - 1
    moved[0] = in_plane(together(sums[0], kernel[k][0])[0])
    got2 = give_to(highs, 2)
    low, high = first_add(k, together(got, highs)[0])
    sums[k - 1] = add(lows, together(got2, high)[0])
    moved[k - 1] = in_plane(sums[k - 1])
    sums[k] = add(low, give_to(high, 2))
    early = jnp.concatenate([moved[at].reshape(2, sizes[at], -1) for at in range(k)], axis=1)
    early, final = together(along_column(together(early, sums[k])[0]), at_once(sums[k], 0))
    crossed = swap(jnp.concatenate([early[1], final[sizes[k] :]], axis=0), 1, n)
    return lay_out(core.reshape(1), early, final, crossed)


def solution(mesh):
    n, m = mesh.shape["tm"], mesh.shape["head"]
    per_device = functools.partial(planes, n=n, m=m) if n == 8 and m == 4 else any_mesh
    tokens = P("tm", "head")
    return jax.shard_map(
        per_device,
        mesh=mesh,
        in_specs=(tokens, tokens, tokens, tokens, P(None, "tm", "head")),
        out_specs=P("head", "tm"),
        check_vma=False,
    )
```

```python
import functools

import jax
import jax.numpy as jnp
from jax import lax
from jax.experimental import pallas as pl
from jax.experimental.pallas import tpu as pltpu
from jax.sharding import PartitionSpec as P

HD = 128
GROUP = 16
UNITS = 12
VMEM_MIB = 32
TILE = 256
WEIGHT = 30
SIZES = (48, 48, 32)

F32 = jnp.float32
BF16 = jnp.bfloat16


def temporal(q_heads, k_heads, v_heads, g_heads):
    scale = 1.0 / q_heads.shape[-1] ** 0.5
    scores = jnp.einsum("fphd,gphd->phfg", q_heads, k_heads, preferred_element_type=F32) * scale
    probs = jax.nn.softmax(scores, axis=-1)
    probs_b = probs.astype(BF16)
    attended = jnp.einsum("phfg,gphd->fphd", probs_b, v_heads, preferred_element_type=F32)
    delta = jnp.transpose(jnp.sum(g_heads.astype(F32) * attended, axis=-1), (1, 2, 0))
    grad_probs = jnp.einsum("fphd,gphd->phfg", g_heads, v_heads, preferred_element_type=F32)
    grad_scores = (probs * (grad_probs - delta[..., None])).astype(BF16)
    grad_value = jnp.einsum("phfg,fphd->gphd", probs_b, g_heads, preferred_element_type=F32)
    grad_query = jnp.einsum("phfg,gphd->fphd", grad_scores, k_heads, preferred_element_type=F32)
    grad_key = jnp.einsum("phfg,fphd->gphd", grad_scores, q_heads, preferred_element_type=F32)
    return (
        (grad_query * scale).astype(BF16),
        (grad_key * scale).astype(BF16),
        grad_value.astype(BF16),
    )


def any_mesh(query, key_in, value, grad_out, weights):
    rows, width = query.shape

    def to_patches(array):
        array = array.reshape(1, rows, width // HD, HD)
        return lax.all_to_all(array, "tm", split_axis=1, concat_axis=0, tiled=True)

    def to_frames(array):
        array = lax.all_to_all(array, "tm", split_axis=0, concat_axis=1, tiled=True)
        return array.reshape(rows, width)

    grads = temporal(*(to_patches(a) for a in (query, key_in, value, grad_out)))
    stacked = jnp.stack([to_frames(g) for g in grads])
    gathered = lax.all_gather(weights, "tm", axis=1, tiled=True)
    partial_sum = jnp.einsum("mic,mtc->it", gathered, stacked, preferred_element_type=F32)
    mine = lax.psum_scatter(partial_sum, "head", scatter_dimension=0, tiled=True)
    return mine.astype(BF16)


def chunk_kernel(info, *refs):
    pieces, (w_own, w_other, keep, pass_on, give, xs, grads, sums, sem) = refs[:5], refs[5:]
    patches, width = pieces[0].shape[2], pieces[0].shape[3]
    features = w_own.shape[1]
    scale = 1.0 / HD**0.5
    log2_scale = scale * 1.4426950408889634
    rows = 8 * GROUP

    per_half = width // 2
    copies = [[], []]
    for half in range(2):
        cs = pl.ds(half * per_half, per_half)
        places = (
            xs.at[:, 0:2, :, cs],
            xs.at[:, 2:4, :, cs],
            xs.at[:, 4:6, :, cs],
            xs.at[0:2, 6:8, :, cs],
            xs.at[2:4, 6:8, :, cs],
        )
        for at, (piece, place) in enumerate(zip(pieces, places)):
            copies[half].append(pltpu.make_async_copy(piece.at[:, :, :, cs], place, sem.at[half, at]))
    for copy in copies[0] + copies[1]:
        copy.start()

    r = lax.broadcasted_iota(jnp.int32, (rows, rows), 0)
    c = lax.broadcasted_iota(jnp.int32, (rows, rows), 1)
    bias = jnp.where((r % GROUP) == (c % GROUP), 0.0, -1e30).astype(F32)
    last = (((1,), (1,)), ((), ()))
    first = (((0,), (0,)), ((), ()))

    def attention(every):
        for start in range(0, len(every), UNITS):
            units = [(pl.ds(g * GROUP, GROUP), pl.ds(h * HD, HD)) for g, h in every[start : start + UNITS]]
            q, k, v, g = ([xs[which, :, ps, cs].reshape(rows, HD) for ps, cs in units] for which in range(4))
            scores = [lax.dot_general(b, a, last, preferred_element_type=F32) + bias for a, b in zip(q, k)]
            grad_probs = [lax.dot_general(b, a, last, preferred_element_type=F32) for a, b in zip(g, v)]
            probs_b, grad_scores = [], []
            for s, gp in zip(scores, grad_probs):
                e = jnp.exp2((s - jnp.max(s, axis=0, keepdims=True)) * log2_scale)
                p = e * (1.0 / jnp.sum(e, axis=0, keepdims=True))
                pb = p.astype(BF16)
                delta = jnp.sum(pb.astype(F32) * gp, axis=0, keepdims=True)
                probs_b.append(pb)
                grad_scores.append((p * (gp - delta)).astype(BF16))
            for at, (ps, cs) in enumerate(units):
                gs, pb = grad_scores[at], probs_b[at]
                gq = lax.dot_general(gs, k[at], first, preferred_element_type=F32) * scale
                gk = jnp.dot(gs, q[at], preferred_element_type=F32) * scale
                gv = jnp.dot(pb, g[at], preferred_element_type=F32)
                for m, grad in enumerate((gq, gk, gv)):
                    grads[m, :, ps, cs] = grad.astype(BF16).reshape(8, GROUP, HD)

    heads = per_half // HD
    for half in range(2):
        for copy in copies[half]:
            copy.wait()
        attention([(g, half * heads + h) for h in range(heads) for g in range(patches // GROUP)])

    for which, ws in enumerate((w_own, w_other)):
        base = (info[4] if which == 0 else 1 - info[4]) * features
        for start in range(0, features, TILE):
            total = None
            for m in range(3):
                flat = grads[m].reshape(8 * patches, width)
                term = lax.dot_general(flat, ws[m, start : start + TILE, :], last, preferred_element_type=F32)
                total = term if total is None else total + term
            sums[:, pl.ds(pl.multiple_of(base + start, TILE), TILE)] = total.astype(BF16)
    part = 2 * patches
    for x in range(4):
        out, row = ((keep, 0), (pass_on, 0), (give, 0), (give, part))[x]
        out[row : row + part, :] = sums[pl.ds(pl.multiple_of(info[x] * part, part), part), :]


def chunk(info, pieces, w_own, w_other):
    patches, width = pieces[0].shape[2], pieces[0].shape[3]
    features = w_own.shape[1]
    vmem = pl.BlockSpec(memory_space=pltpu.VMEM)
    return pl.pallas_call(
        chunk_kernel,
        in_specs=[pl.BlockSpec(memory_space=pltpu.SMEM)] + [pl.BlockSpec(memory_space=pl.ANY)] * 5 + [vmem] * 2,
        out_specs=[vmem] * 3,
        out_shape=[jax.ShapeDtypeStruct((n * patches, 2 * features), BF16) for n in (2, 2, 4)],
        scratch_shapes=[
            pltpu.VMEM((4, 8, patches, width), BF16),
            pltpu.VMEM((3, 8, patches, width), BF16),
            pltpu.VMEM((8 * patches, 2 * features), BF16),
            pltpu.SemaphoreType.DMA((2, 5)),
        ],
        compiler_params=pltpu.CompilerParams(vmem_limit_bytes=VMEM_MIB * 1024 * 1024),
        cost_estimate=pl.CostEstimate(
            flops=WEIGHT * (96 * patches * width * features + 80 * patches * 8 * GROUP * width),
            bytes_accessed=WEIGHT * (12 * features * width + 112 * patches * width),
            transcendentals=WEIGHT * (8 * patches * 8 * GROUP * width // HD),
        ),
        name="attention_and_product",
    )(info, *pieces, w_own, w_other)


def lay_kernel(core, early, final, crossed, out, kept_buffer, crossed_buffer, sem):
    half, size = crossed.shape[0], early.shape[1]
    copies = [
        pltpu.make_async_copy(early.at[0], kept_buffer.at[0:size], sem.at[0]),
        pltpu.make_async_copy(final.at[0 : half - size], kept_buffer.at[size:half], sem.at[1]),
        pltpu.make_async_copy(crossed, crossed_buffer, sem.at[2]),
    ]
    for copy in copies:
        copy.start()
    copies[0].wait()
    copies[1].wait()
    out[:, pl.ds(pl.multiple_of(core[0] * half, half), half)] = kept_buffer[...].T
    copies[2].wait()
    out[:, pl.ds(pl.multiple_of((1 - core[0]) * half, half), half)] = crossed_buffer[...].T


def lay_out(core, early, final, crossed):
    half, features = crossed.shape
    return pl.pallas_call(
        lay_kernel,
        in_specs=[pl.BlockSpec(memory_space=pltpu.SMEM)] + [pl.BlockSpec(memory_space=pl.ANY)] * 3,
        out_specs=pl.BlockSpec(memory_space=pltpu.VMEM),
        out_shape=jax.ShapeDtypeStruct((features, 2 * half), BF16),
        scratch_shapes=[
            pltpu.VMEM((half, features), BF16),
            pltpu.VMEM((half, features), BF16),
            pltpu.SemaphoreType.DMA((3,)),
        ],
        compiler_params=pltpu.CompilerParams(vmem_limit_bytes=60 * 1024 * 1024),
        name="lay_out",
    )(core, early, final, crossed)


def swap(array, bit, n):
    return lax.ppermute(array, "tm", [(i, i ^ bit) for i in range(n)])


def after(array, *others):
    return lax.optimization_barrier((array, *others))[0]


COLUMN = ((0, 1, 2, 3), (2, 3, 0, 1), (3, 2, 1, 0), (1, 0, 3, 2))


def planes(query, key_in, value, grad_out, weights, *, n, m):
    rows, width = query.shape
    half = rows // 2
    chip, core = lax.axis_index("tm") // 2, lax.axis_index("tm") % 2
    plane = lax.axis_index("head")
    table = [[[COLUMN[r][z ^ x] ^ r for x in (0, 2, 1, 3)] for z in range(m)] for r in range(n // 2)]
    info = jnp.append(jnp.asarray(table, jnp.int32)[chip, plane], core)

    def together(*arrays):
        return lax.optimization_barrier(arrays)

    sizes = SIZES
    count = len(sizes)

    def rows_of(which, start, stop):
        arrays = (query, key_in, value, grad_out)
        return jnp.stack([lax.dynamic_slice_in_dim(a, which * half + start, stop - start, 0) for a in arrays])

    def meet(start, stop, *gate):
        theirs = swap(together(rows_of(1 - core, start, stop), *gate)[0], 1, n)
        return jnp.stack([rows_of(core, start, stop), theirs], axis=1), theirs

    begin, theirs = meet(0, sizes[0])
    rest, _ = meet(sizes[0], half, theirs)
    other = swap(after(weights, theirs), 1, n)
    own = [begin] + [
        lax.slice_in_dim(rest, sum(sizes[1:i]), sum(sizes[1 : i + 1]), axis=2) for i in range(1, count)
    ]

    def move(array, to):
        pairs = [(t * m + z, to(t // 2, t % 2, z)) for t in range(n) for z in range(m)]
        return lax.ppermute(array, ("tm", "head"), pairs)

    def in_plane(array):
        return move(array, lambda r, c, z: (COLUMN[r][z] * 2 + c) * m + z)

    def along_column(array):
        source = {(COLUMN[r][z], z): r for r in range(n // 2) for z in range(m)}
        return move(array, lambda s, c, z: (s * 2 + c) * m + source[s, z])

    def at_once(array, bit):
        return move(array, lambda r, c, z: (COLUMN[r][z] * 2 + (c ^ bit)) * m + r)

    def give_to(array, bit):
        return lax.ppermute(array, "head", [(z, z ^ bit) for z in range(m)])

    def add(a, b):
        return (a.astype(F32) + b.astype(F32)).astype(BF16)

    kernel, sums, moved = {}, {}, {}

    def first_add(k, got):
        keep, pass_on, _ = kernel[k]
        quarter = 2 * sizes[k]
        return add(keep, got[:quarter]), add(pass_on, got[quarter:])

    x1, x2 = swap(own[0], 2, n), swap(own[0], 4, n)
    low = high = None
    for k in range(count):
        gate = [kernel[k - 1][0]] if k >= 1 else []
        if k >= 2:
            sums[k - 2] = add(lows, give_to(highs, 2))
            gate += [sums[k - 2]]
        g1, g2 = together(x1, x2, *gate)[:2]
        g1, g2 = g1[:2], g2[2:]
        last = k == count - 1
        if not last:
            following = together(own[k + 1], g1, g2)[0]
            n1, n2 = swap(following, 2, n), swap(following, 4, n)
        pieces = (own[k], x1, x2, swap(g1, 4, n), swap(g2, 2, n))
        gate = []
        if k >= 1 and not last:
            lows, highs = first_add(k - 1, got)
            gate += [highs]
        pieces = together(*pieces, *gate)[:5]
        kernel[k] = chunk(info, pieces, weights, other)
        if last:
            lows, highs = first_add(k - 1, together(got, kernel[k][0])[0])
        got = give_to(kernel[k][2], 1)
        if not last:
            x1, x2 = n1, n2

    k = count - 1
    moved[0] = in_plane(together(sums[0], kernel[k][0])[0])
    got2 = give_to(highs, 2)
    low, high = first_add(k, together(got, highs)[0])
    sums[k - 1] = add(lows, together(got2, high)[0])
    moved[k - 1] = in_plane(sums[k - 1])
    sums[k] = add(low, give_to(high, 2))
    early = jnp.concatenate([moved[at].reshape(2, sizes[at], -1) for at in range(k)], axis=1)
    early, final = together(along_column(together(early, sums[k])[0]), at_once(sums[k], 0))
    crossed = swap(jnp.concatenate([early[1], final[sizes[k] :]], axis=0), 1, n)
    return lay_out(core.reshape(1), early, final, crossed)


def solution(mesh):
    n, m = mesh.shape["tm"], mesh.shape["head"]
    per_device = functools.partial(planes, n=n, m=m) if n == 8 and m == 4 else any_mesh
    tokens = P("tm", "head")
    return jax.shard_map(
        per_device,
        mesh=mesh,
        in_specs=(tokens, tokens, tokens, tokens, P(None, "tm", "head")),
        out_specs=P("head", "tm"),
        check_vma=False,
    )
```

```python
import functools

import jax
import jax.numpy as jnp
from jax import lax
from jax.experimental import pallas as pl
from jax.experimental.pallas import tpu as pltpu
from jax.sharding import PartitionSpec as P

HD = 128
GROUP = 16
UNITS = 12
VMEM_MIB = 32
TILE = 256
WEIGHT = 30
SIZES = (48, 48, 32)

F32 = jnp.float32
BF16 = jnp.bfloat16


def temporal(q_heads, k_heads, v_heads, g_heads):
    scale = 1.0 / q_heads.shape[-1] ** 0.5
    scores = jnp.einsum("fphd,gphd->phfg", q_heads, k_heads, preferred_element_type=F32) * scale
    probs = jax.nn.softmax(scores, axis=-1)
    probs_b = probs.astype(BF16)
    attended = jnp.einsum("phfg,gphd->fphd", probs_b, v_heads, preferred_element_type=F32)
    delta = jnp.transpose(jnp.sum(g_heads.astype(F32) * attended, axis=-1), (1, 2, 0))
    grad_probs = jnp.einsum("fphd,gphd->phfg", g_heads, v_heads, preferred_element_type=F32)
    grad_scores = (probs * (grad_probs - delta[..., None])).astype(BF16)
    grad_value = jnp.einsum("phfg,fphd->gphd", probs_b, g_heads, preferred_element_type=F32)
    grad_query = jnp.einsum("phfg,gphd->fphd", grad_scores, k_heads, preferred_element_type=F32)
    grad_key = jnp.einsum("phfg,fphd->gphd", grad_scores, q_heads, preferred_element_type=F32)
    return (
        (grad_query * scale).astype(BF16),
        (grad_key * scale).astype(BF16),
        grad_value.astype(BF16),
    )


def any_mesh(query, key_in, value, grad_out, weights):
    rows, width = query.shape

    def to_patches(array):
        array = array.reshape(1, rows, width // HD, HD)
        return lax.all_to_all(array, "tm", split_axis=1, concat_axis=0, tiled=True)

    def to_frames(array):
        array = lax.all_to_all(array, "tm", split_axis=0, concat_axis=1, tiled=True)
        return array.reshape(rows, width)

    grads = temporal(*(to_patches(a) for a in (query, key_in, value, grad_out)))
    stacked = jnp.stack([to_frames(g) for g in grads])
    gathered = lax.all_gather(weights, "tm", axis=1, tiled=True)
    partial_sum = jnp.einsum("mic,mtc->it", gathered, stacked, preferred_element_type=F32)
    mine = lax.psum_scatter(partial_sum, "head", scatter_dimension=0, tiled=True)
    return mine.astype(BF16)


def chunk_kernel(info, *refs):
    pieces, (w_own, w_other, keep, pass_on, give, xs, grads, sums, sem) = refs[:5], refs[5:]
    patches, width = pieces[0].shape[2], pieces[0].shape[3]
    features = w_own.shape[1]
    scale = 1.0 / HD**0.5
    log2_scale = scale * 1.4426950408889634
    rows = 8 * GROUP

    per_half = width // 2
    copies = [[], []]
    for half in range(2):
        cs = pl.ds(half * per_half, per_half)
        places = (
            xs.at[:, 0:2, :, cs],
            xs.at[:, 2:4, :, cs],
            xs.at[:, 4:6, :, cs],
            xs.at[0:2, 6:8, :, cs],
            xs.at[2:4, 6:8, :, cs],
        )
        for at, (piece, place) in enumerate(zip(pieces, places)):
            copies[half].append(pltpu.make_async_copy(piece.at[:, :, :, cs], place, sem.at[half, at]))
    for copy in copies[0] + copies[1]:
        copy.start()

    r = lax.broadcasted_iota(jnp.int32, (rows, rows), 0)
    c = lax.broadcasted_iota(jnp.int32, (rows, rows), 1)
    bias = jnp.where((r % GROUP) == (c % GROUP), 0.0, -1e30).astype(F32)
    last = (((1,), (1,)), ((), ()))
    first = (((0,), (0,)), ((), ()))

    def attention(every):
        for start in range(0, len(every), UNITS):
            units = [(pl.ds(g * GROUP, GROUP), pl.ds(h * HD, HD)) for g, h in every[start : start + UNITS]]
            q, k, v, g = ([xs[which, :, ps, cs].reshape(rows, HD) for ps, cs in units] for which in range(4))
            scores = [lax.dot_general(b, a, last, preferred_element_type=F32) + bias for a, b in zip(q, k)]
            grad_probs = [lax.dot_general(b, a, last, preferred_element_type=F32) for a, b in zip(g, v)]
            probs_b, grad_scores = [], []
            for s, gp in zip(scores, grad_probs):
                e = jnp.exp2((s - jnp.max(s, axis=0, keepdims=True)) * log2_scale)
                p = e * (1.0 / jnp.sum(e, axis=0, keepdims=True))
                pb = p.astype(BF16)
                delta = jnp.sum(pb.astype(F32) * gp, axis=0, keepdims=True)
                probs_b.append(pb)
                grad_scores.append((p * (gp - delta)).astype(BF16))
            for at, (ps, cs) in enumerate(units):
                gs, pb = grad_scores[at], probs_b[at]
                gq = lax.dot_general(gs, k[at], first, preferred_element_type=F32) * scale
                gk = jnp.dot(gs, q[at], preferred_element_type=F32) * scale
                gv = jnp.dot(pb, g[at], preferred_element_type=F32)
                for m, grad in enumerate((gq, gk, gv)):
                    grads[m, :, ps, cs] = grad.astype(BF16).reshape(8, GROUP, HD)

    heads = per_half // HD
    for half in range(2):
        for copy in copies[half]:
            copy.wait()
        attention([(g, half * heads + h) for h in range(heads) for g in range(patches // GROUP)])

    for which, ws in enumerate((w_own, w_other)):
        base = (info[4] if which == 0 else 1 - info[4]) * features
        for start in range(0, features, TILE):
            total = None
            for m in range(3):
                flat = grads[m].reshape(8 * patches, width)
                term = lax.dot_general(flat, ws[m, start : start + TILE, :], last, preferred_element_type=F32)
                total = term if total is None else total + term
            sums[:, pl.ds(pl.multiple_of(base + start, TILE), TILE)] = total.astype(BF16)
    part = 2 * patches
    for x in range(4):
        out, row = ((keep, 0), (pass_on, 0), (give, 0), (give, part))[x]
        out[row : row + part, :] = sums[pl.ds(pl.multiple_of(info[x] * part, part), part), :]


def chunk(info, pieces, w_own, w_other):
    patches, width = pieces[0].shape[2], pieces[0].shape[3]
    features = w_own.shape[1]
    vmem = pl.BlockSpec(memory_space=pltpu.VMEM)
    return pl.pallas_call(
        chunk_kernel,
        in_specs=[pl.BlockSpec(memory_space=pltpu.SMEM)] + [pl.BlockSpec(memory_space=pl.ANY)] * 5 + [vmem] * 2,
        out_specs=[vmem] * 3,
        out_shape=[jax.ShapeDtypeStruct((n * patches, 2 * features), BF16) for n in (2, 2, 4)],
        scratch_shapes=[
            pltpu.VMEM((4, 8, patches, width), BF16),
            pltpu.VMEM((3, 8, patches, width), BF16),
            pltpu.VMEM((8 * patches, 2 * features), BF16),
            pltpu.SemaphoreType.DMA((2, 5)),
        ],
        compiler_params=pltpu.CompilerParams(vmem_limit_bytes=VMEM_MIB * 1024 * 1024),
        cost_estimate=pl.CostEstimate(
            flops=WEIGHT * (96 * patches * width * features + 80 * patches * 8 * GROUP * width),
            bytes_accessed=WEIGHT * (12 * features * width + 112 * patches * width),
            transcendentals=WEIGHT * (8 * patches * 8 * GROUP * width // HD),
        ),
        name="attention_and_product",
    )(info, *pieces, w_own, w_other)


def lay_kernel(core, early, final, crossed, out, kept_buffer, crossed_buffer, sem):
    half, size = crossed.shape[0], early.shape[1]
    copies = [
        pltpu.make_async_copy(early.at[0], kept_buffer.at[0:size], sem.at[0]),
        pltpu.make_async_copy(final.at[0 : half - size], kept_buffer.at[size:half], sem.at[1]),
        pltpu.make_async_copy(crossed, crossed_buffer, sem.at[2]),
    ]
    for copy in copies:
        copy.start()
    copies[0].wait()
    copies[1].wait()
    out[:, pl.ds(pl.multiple_of(core[0] * half, half), half)] = kept_buffer[...].T
    copies[2].wait()
    out[:, pl.ds(pl.multiple_of((1 - core[0]) * half, half), half)] = crossed_buffer[...].T


def lay_out(core, early, final, crossed):
    half, features = crossed.shape
    return pl.pallas_call(
        lay_kernel,
        in_specs=[pl.BlockSpec(memory_space=pltpu.SMEM)] + [pl.BlockSpec(memory_space=pl.ANY)] * 3,
        out_specs=pl.BlockSpec(memory_space=pltpu.VMEM),
        out_shape=jax.ShapeDtypeStruct((features, 2 * half), BF16),
        scratch_shapes=[
            pltpu.VMEM((half, features), BF16),
            pltpu.VMEM((half, features), BF16),
            pltpu.SemaphoreType.DMA((3,)),
        ],
        compiler_params=pltpu.CompilerParams(vmem_limit_bytes=60 * 1024 * 1024),
        name="lay_out",
    )(core, early, final, crossed)


def swap(array, bit, n):
    return lax.ppermute(array, "tm", [(i, i ^ bit) for i in range(n)])


def after(array, *others):
    return lax.optimization_barrier((array, *others))[0]


COLUMN = ((0, 1, 2, 3), (2, 3, 0, 1), (3, 2, 1, 0), (1, 0, 3, 2))


def planes(query, key_in, value, grad_out, weights, *, n, m):
    rows, width = query.shape
    half = rows // 2
    chip, core = lax.axis_index("tm") // 2, lax.axis_index("tm") % 2
    plane = lax.axis_index("head")
    table = [[[COLUMN[r][z ^ x] ^ r for x in (0, 2, 1, 3)] for z in range(m)] for r in range(n // 2)]
    info = jnp.append(jnp.asarray(table, jnp.int32)[chip, plane], core)

    def together(*arrays):
        return lax.optimization_barrier(arrays)

    sizes = SIZES
    count = len(sizes)

    def rows_of(which, start, stop):
        arrays = (query, key_in, value, grad_out)
        return jnp.stack([lax.dynamic_slice_in_dim(a, which * half + start, stop - start, 0) for a in arrays])

    def meet(start, stop, *gate):
        theirs = swap(together(rows_of(1 - core, start, stop), *gate)[0], 1, n)
        return jnp.stack([rows_of(core, start, stop), theirs], axis=1), theirs

    begin, theirs = meet(0, sizes[0])
    rest, _ = meet(sizes[0], half, theirs)
    other = swap(after(weights, theirs), 1, n)
    own = [begin] + [
        lax.slice_in_dim(rest, sum(sizes[1:i]), sum(sizes[1 : i + 1]), axis=2) for i in range(1, count)
    ]

    def move(array, to):
        pairs = [(t * m + z, to(t // 2, t % 2, z)) for t in range(n) for z in range(m)]
        return lax.ppermute(array, ("tm", "head"), pairs)

    def in_plane(array):
        return move(array, lambda r, c, z: (COLUMN[r][z] * 2 + c) * m + z)

    def along_column(array):
        source = {(COLUMN[r][z], z): r for r in range(n // 2) for z in range(m)}
        return move(array, lambda s, c, z: (s * 2 + c) * m + source[s, z])

    def at_once(array, bit):
        return move(array, lambda r, c, z: (COLUMN[r][z] * 2 + (c ^ bit)) * m + r)

    def give_to(array, bit):
        return lax.ppermute(array, "head", [(z, z ^ bit) for z in range(m)])

    def add(a, b):
        return (a.astype(F32) + b.astype(F32)).astype(BF16)

    kernel, sums, moved = {}, {}, {}

    def first_add(k, got):
        keep, pass_on, _ = kernel[k]
        quarter = 2 * sizes[k]
        return add(keep, got[:quarter]), add(pass_on, got[quarter:])

    x1, x2 = swap(own[0], 2, n), swap(own[0], 4, n)
    low = high = None
    for k in range(count):
        gate = [kernel[k - 1][0]] if k >= 1 else []
        if k >= 2:
            sums[k - 2] = add(lows, give_to(highs, 2))
            gate += [sums[k - 2]]
        g1, g2 = together(x1, x2, *gate)[:2]
        g1, g2 = g1[:2], g2[2:]
        last = k == count - 1
        if not last:
            following = together(own[k + 1], g1, g2)[0]
            n1, n2 = swap(following, 2, n), swap(following, 4, n)
        pieces = (own[k], x1, x2, swap(g1, 4, n), swap(g2, 2, n))
        gate = []
        if k >= 1 and not last:
            lows, highs = first_add(k - 1, got)
            gate += [highs]
        pieces = together(*pieces, *gate)[:5]
        kernel[k] = chunk(info, pieces, weights, other)
        if last:
            lows, highs = first_add(k - 1, together(got, kernel[k][0])[0])
        got = give_to(kernel[k][2], 1)
        if not last:
            x1, x2 = n1, n2

    k = count - 1
    moved[0] = in_plane(together(sums[0], kernel[k][0], highs)[0])
    got2 = give_to(highs, 2)
    low, high = first_add(k, together(got, highs)[0])
    sums[k - 1] = add(lows, together(got2, high)[0])
    moved[k - 1] = in_plane(sums[k - 1])
    sums[k] = add(low, give_to(high, 2))
    early = jnp.concatenate([moved[at].reshape(2, sizes[at], -1) for at in range(k)], axis=1)
    early, final = together(along_column(together(early, sums[k])[0]), at_once(sums[k], 0))
    crossed = swap(jnp.concatenate([early[1], final[sizes[k] :]], axis=0), 1, n)
    return lay_out(core.reshape(1), early, final, crossed)


def solution(mesh):
    n, m = mesh.shape["tm"], mesh.shape["head"]
    per_device = functools.partial(planes, n=n, m=m) if n == 8 and m == 4 else any_mesh
    tokens = P("tm", "head")
    return jax.shard_map(
        per_device,
        mesh=mesh,
        in_specs=(tokens, tokens, tokens, tokens, P(None, "tm", "head")),
        out_specs=P("head", "tm"),
        check_vma=False,
    )
```

```python
import functools

import jax
import jax.numpy as jnp
from jax import lax
from jax.experimental import pallas as pl
from jax.experimental.pallas import tpu as pltpu
from jax.sharding import PartitionSpec as P

HD = 128
GROUP = 16
UNITS = 24
VMEM_MIB = 32
TILE = 256
WEIGHT = 15
SIZES = (48, 48, 32)

F32 = jnp.float32
BF16 = jnp.bfloat16


def temporal(q_heads, k_heads, v_heads, g_heads):
    scale = 1.0 / q_heads.shape[-1] ** 0.5
    scores = jnp.einsum("fphd,gphd->phfg", q_heads, k_heads, preferred_element_type=F32) * scale
    probs = jax.nn.softmax(scores, axis=-1)
    probs_b = probs.astype(BF16)
    attended = jnp.einsum("phfg,gphd->fphd", probs_b, v_heads, preferred_element_type=F32)
    delta = jnp.transpose(jnp.sum(g_heads.astype(F32) * attended, axis=-1), (1, 2, 0))
    grad_probs = jnp.einsum("fphd,gphd->phfg", g_heads, v_heads, preferred_element_type=F32)
    grad_scores = (probs * (grad_probs - delta[..., None])).astype(BF16)
    grad_value = jnp.einsum("phfg,fphd->gphd", probs_b, g_heads, preferred_element_type=F32)
    grad_query = jnp.einsum("phfg,gphd->fphd", grad_scores, k_heads, preferred_element_type=F32)
    grad_key = jnp.einsum("phfg,fphd->gphd", grad_scores, q_heads, preferred_element_type=F32)
    return (
        (grad_query * scale).astype(BF16),
        (grad_key * scale).astype(BF16),
        grad_value.astype(BF16),
    )


def any_mesh(query, key_in, value, grad_out, weights):
    rows, width = query.shape

    def to_patches(array):
        array = array.reshape(1, rows, width // HD, HD)
        return lax.all_to_all(array, "tm", split_axis=1, concat_axis=0, tiled=True)

    def to_frames(array):
        array = lax.all_to_all(array, "tm", split_axis=0, concat_axis=1, tiled=True)
        return array.reshape(rows, width)

    grads = temporal(*(to_patches(a) for a in (query, key_in, value, grad_out)))
    stacked = jnp.stack([to_frames(g) for g in grads])
    gathered = lax.all_gather(weights, "tm", axis=1, tiled=True)
    partial_sum = jnp.einsum("mic,mtc->it", gathered, stacked, preferred_element_type=F32)
    mine = lax.psum_scatter(partial_sum, "head", scatter_dimension=0, tiled=True)
    return mine.astype(BF16)


def chunk_kernel(info, *refs):
    pieces, (w_own, w_other, keep, pass_on, give, xs, grads, sums, sem) = refs[:5], refs[5:]
    patches, width = pieces[0].shape[2], pieces[0].shape[3]
    features = w_own.shape[1]
    scale = 1.0 / HD**0.5
    log2_scale = scale * 1.4426950408889634
    rows = 8 * GROUP

    per_half = width // 2
    copies = [[], []]
    for half in range(2):
        cs = pl.ds(half * per_half, per_half)
        places = (
            xs.at[:, 0:2, :, cs],
            xs.at[:, 2:4, :, cs],
            xs.at[:, 4:6, :, cs],
            xs.at[0:2, 6:8, :, cs],
            xs.at[2:4, 6:8, :, cs],
        )
        for at, (piece, place) in enumerate(zip(pieces, places)):
            copies[half].append(pltpu.make_async_copy(piece.at[:, :, :, cs], place, sem.at[half, at]))
    for copy in copies[0] + copies[1]:
        copy.start()

    r = lax.broadcasted_iota(jnp.int32, (rows, rows), 0)
    c = lax.broadcasted_iota(jnp.int32, (rows, rows), 1)
    bias = jnp.where((r % GROUP) == (c % GROUP), 0.0, -1e30).astype(F32)
    last = (((1,), (1,)), ((), ()))
    first = (((0,), (0,)), ((), ()))

    def attention(every):
        for start in range(0, len(every), UNITS):
            units = [(pl.ds(g * GROUP, GROUP), pl.ds(h * HD, HD)) for g, h in every[start : start + UNITS]]
            q, k, v, g = ([xs[which, :, ps, cs].reshape(rows, HD) for ps, cs in units] for which in range(4))
            scores = [lax.dot_general(b, a, last, preferred_element_type=F32) + bias for a, b in zip(q, k)]
            grad_probs = [lax.dot_general(b, a, last, preferred_element_type=F32) for a, b in zip(g, v)]
            probs_b, grad_scores = [], []
            for s, gp in zip(scores, grad_probs):
                e = jnp.exp2((s - jnp.max(s, axis=0, keepdims=True)) * log2_scale)
                p = e * (1.0 / jnp.sum(e, axis=0, keepdims=True))
                pb = p.astype(BF16)
                delta = jnp.sum(pb.astype(F32) * gp, axis=0, keepdims=True)
                probs_b.append(pb)
                grad_scores.append((p * (gp - delta)).astype(BF16))
            for at, (ps, cs) in enumerate(units):
                gs, pb = grad_scores[at], probs_b[at]
                gq = lax.dot_general(gs, k[at], first, preferred_element_type=F32) * scale
                gk = jnp.dot(gs, q[at], preferred_element_type=F32) * scale
                gv = jnp.dot(pb, g[at], preferred_element_type=F32)
                for m, grad in enumerate((gq, gk, gv)):
                    grads[m, :, ps, cs] = grad.astype(BF16).reshape(8, GROUP, HD)

    heads = per_half // HD
    for half in range(2):
        for copy in copies[half]:
            copy.wait()
        attention([(g, half * heads + h) for h in range(heads) for g in range(patches // GROUP)])

    for which, ws in enumerate((w_own, w_other)):
        base = (info[4] if which == 0 else 1 - info[4]) * features
        for start in range(0, features, TILE):
            total = None
            for m in range(3):
                flat = grads[m].reshape(8 * patches, width)
                term = lax.dot_general(flat, ws[m, start : start + TILE, :], last, preferred_element_type=F32)
                total = term if total is None else total + term
            sums[:, pl.ds(pl.multiple_of(base + start, TILE), TILE)] = total.astype(BF16)
    part = 2 * patches
    for x in range(4):
        out, row = ((keep, 0), (pass_on, 0), (give, 0), (give, part))[x]
        out[row : row + part, :] = sums[pl.ds(pl.multiple_of(info[x] * part, part), part), :]


def chunk(info, pieces, w_own, w_other):
    patches, width = pieces[0].shape[2], pieces[0].shape[3]
    features = w_own.shape[1]
    vmem = pl.BlockSpec(memory_space=pltpu.VMEM)
    return pl.pallas_call(
        chunk_kernel,
        in_specs=[pl.BlockSpec(memory_space=pltpu.SMEM)] + [pl.BlockSpec(memory_space=pl.ANY)] * 5 + [vmem] * 2,
        out_specs=[vmem] * 3,
        out_shape=[jax.ShapeDtypeStruct((n * patches, 2 * features), BF16) for n in (2, 2, 4)],
        scratch_shapes=[
            pltpu.VMEM((4, 8, patches, width), BF16),
            pltpu.VMEM((3, 8, patches, width), BF16),
            pltpu.VMEM((8 * patches, 2 * features), BF16),
            pltpu.SemaphoreType.DMA((2, 5)),
        ],
        compiler_params=pltpu.CompilerParams(vmem_limit_bytes=VMEM_MIB * 1024 * 1024),
        cost_estimate=pl.CostEstimate(
            flops=WEIGHT * (96 * patches * width * features + 80 * patches * 8 * GROUP * width),
            bytes_accessed=WEIGHT * (12 * features * width + 112 * patches * width),
            transcendentals=WEIGHT * (8 * patches * 8 * GROUP * width // HD),
        ),
        name="attention_and_product",
    )(info, *pieces, w_own, w_other)


def lay_kernel(core, early, final, crossed, out, kept_buffer, crossed_buffer, sem):
    half, size = crossed.shape[0], early.shape[1]
    copies = [
        pltpu.make_async_copy(early.at[0], kept_buffer.at[0:size], sem.at[0]),
        pltpu.make_async_copy(final.at[0 : half - size], kept_buffer.at[size:half], sem.at[1]),
        pltpu.make_async_copy(crossed, crossed_buffer, sem.at[2]),
    ]
    for copy in copies:
        copy.start()
    copies[0].wait()
    copies[1].wait()
    out[:, pl.ds(pl.multiple_of(core[0] * half, half), half)] = kept_buffer[...].T
    copies[2].wait()
    out[:, pl.ds(pl.multiple_of((1 - core[0]) * half, half), half)] = crossed_buffer[...].T


def lay_out(core, early, final, crossed):
    half, features = crossed.shape
    return pl.pallas_call(
        lay_kernel,
        in_specs=[pl.BlockSpec(memory_space=pltpu.SMEM)] + [pl.BlockSpec(memory_space=pl.ANY)] * 3,
        out_specs=pl.BlockSpec(memory_space=pltpu.VMEM),
        out_shape=jax.ShapeDtypeStruct((features, 2 * half), BF16),
        scratch_shapes=[
            pltpu.VMEM((half, features), BF16),
            pltpu.VMEM((half, features), BF16),
            pltpu.SemaphoreType.DMA((3,)),
        ],
        compiler_params=pltpu.CompilerParams(vmem_limit_bytes=60 * 1024 * 1024),
        name="lay_out",
    )(core, early, final, crossed)


def swap(array, bit, n):
    return lax.ppermute(array, "tm", [(i, i ^ bit) for i in range(n)])


def after(array, *others):
    return lax.optimization_barrier((array, *others))[0]


COLUMN = ((0, 1, 2, 3), (2, 3, 0, 1), (3, 2, 1, 0), (1, 0, 3, 2))


def planes(query, key_in, value, grad_out, weights, *, n, m):
    rows, width = query.shape
    half = rows // 2
    chip, core = lax.axis_index("tm") // 2, lax.axis_index("tm") % 2
    plane = lax.axis_index("head")
    table = [[[COLUMN[r][z ^ x] ^ r for x in (0, 2, 1, 3)] for z in range(m)] for r in range(n // 2)]
    info = jnp.append(jnp.asarray(table, jnp.int32)[chip, plane], core)

    def together(*arrays):
        return lax.optimization_barrier(arrays)

    sizes = SIZES
    count = len(sizes)

    def rows_of(which, start, stop):
        arrays = (query, key_in, value, grad_out)
        return jnp.stack([lax.dynamic_slice_in_dim(a, which * half + start, stop - start, 0) for a in arrays])

    def meet(start, stop, *gate):
        theirs = swap(together(rows_of(1 - core, start, stop), *gate)[0], 1, n)
        return jnp.stack([rows_of(core, start, stop), theirs], axis=1), theirs

    begin, theirs = meet(0, sizes[0])
    rest, _ = meet(sizes[0], half, theirs)
    other = swap(after(weights, theirs), 1, n)
    own = [begin] + [
        lax.slice_in_dim(rest, sum(sizes[1:i]), sum(sizes[1 : i + 1]), axis=2) for i in range(1, count)
    ]

    def move(array, to):
        pairs = [(t * m + z, to(t // 2, t % 2, z)) for t in range(n) for z in range(m)]
        return lax.ppermute(array, ("tm", "head"), pairs)

    def in_plane(array):
        return move(array, lambda r, c, z: (COLUMN[r][z] * 2 + c) * m + z)

    def along_column(array):
        source = {(COLUMN[r][z], z): r for r in range(n // 2) for z in range(m)}
        return move(array, lambda s, c, z: (s * 2 + c) * m + source[s, z])

    def at_once(array, bit):
        return move(array, lambda r, c, z: (COLUMN[r][z] * 2 + (c ^ bit)) * m + r)

    def give_to(array, bit):
        return lax.ppermute(array, "head", [(z, z ^ bit) for z in range(m)])

    def add(a, b):
        return (a.astype(F32) + b.astype(F32)).astype(BF16)

    kernel, sums, moved = {}, {}, {}

    def first_add(k, got):
        keep, pass_on, _ = kernel[k]
        quarter = 2 * sizes[k]
        return add(keep, got[:quarter]), add(pass_on, got[quarter:])

    x1, x2 = swap(own[0], 2, n), swap(own[0], 4, n)
    low = high = None
    for k in range(count):
        gate = [kernel[k - 1][0]] if k >= 1 else []
        if k >= 2:
            sums[k - 2] = add(lows, give_to(highs, 2))
            gate += [sums[k - 2]]
        g1, g2 = together(x1, x2, *gate)[:2]
        g1, g2 = g1[:2], g2[2:]
        last = k == count - 1
        if not last:
            following = together(own[k + 1], g1, g2)[0]
            n1, n2 = swap(following, 2, n), swap(following, 4, n)
        pieces = (own[k], x1, x2, swap(g1, 4, n), swap(g2, 2, n))
        gate = []
        if k >= 1 and not last:
            lows, highs = first_add(k - 1, got)
            gate += [highs]
        pieces = together(*pieces, *gate)[:5]
        kernel[k] = chunk(info, pieces, weights, other)
        if last:
            lows, highs = first_add(k - 1, together(got, kernel[k][0])[0])
        got = give_to(kernel[k][2], 1)
        if not last:
            x1, x2 = n1, n2

    k = count - 1
    moved[0] = in_plane(together(sums[0], kernel[k][0], highs)[0])
    got2 = give_to(highs, 2)
    low, high = first_add(k, together(got, highs)[0])
    sums[k - 1] = add(lows, together(got2, high)[0])
    moved[k - 1] = in_plane(sums[k - 1])
    sums[k] = add(low, give_to(high, 2))
    early = jnp.concatenate([moved[at].reshape(2, sizes[at], -1) for at in range(k)], axis=1)
    early, final = together(along_column(together(early, sums[k])[0]), at_once(sums[k], 0))
    crossed = swap(jnp.concatenate([early[1], final[sizes[k] :]], axis=0), 1, n)
    return lay_out(core.reshape(1), early, final, crossed)


def solution(mesh):
    n, m = mesh.shape["tm"], mesh.shape["head"]
    per_device = functools.partial(planes, n=n, m=m) if n == 8 and m == 4 else any_mesh
    tokens = P("tm", "head")
    return jax.shard_map(
        per_device,
        mesh=mesh,
        in_specs=(tokens, tokens, tokens, tokens, P(None, "tm", "head")),
        out_specs=P("head", "tm"),
        check_vma=False,
    )
```

```python
import functools

import jax
import jax.numpy as jnp
from jax import lax
from jax.experimental import pallas as pl
from jax.experimental.pallas import tpu as pltpu
from jax.sharding import PartitionSpec as P

HD = 128
GROUP = 16
UNITS = 12
VMEM_MIB = 32
TILE = 256
WEIGHT = 30
SIZES = (48, 48, 32)

F32 = jnp.float32
BF16 = jnp.bfloat16


def temporal(q_heads, k_heads, v_heads, g_heads):
    scale = 1.0 / q_heads.shape[-1] ** 0.5
    scores = jnp.einsum("fphd,gphd->phfg", q_heads, k_heads, preferred_element_type=F32) * scale
    probs = jax.nn.softmax(scores, axis=-1)
    probs_b = probs.astype(BF16)
    attended = jnp.einsum("phfg,gphd->fphd", probs_b, v_heads, preferred_element_type=F32)
    delta = jnp.transpose(jnp.sum(g_heads.astype(F32) * attended, axis=-1), (1, 2, 0))
    grad_probs = jnp.einsum("fphd,gphd->phfg", g_heads, v_heads, preferred_element_type=F32)
    grad_scores = (probs * (grad_probs - delta[..., None])).astype(BF16)
    grad_value = jnp.einsum("phfg,fphd->gphd", probs_b, g_heads, preferred_element_type=F32)
    grad_query = jnp.einsum("phfg,gphd->fphd", grad_scores, k_heads, preferred_element_type=F32)
    grad_key = jnp.einsum("phfg,fphd->gphd", grad_scores, q_heads, preferred_element_type=F32)
    return (
        (grad_query * scale).astype(BF16),
        (grad_key * scale).astype(BF16),
        grad_value.astype(BF16),
    )


def any_mesh(query, key_in, value, grad_out, weights):
    rows, width = query.shape

    def to_patches(array):
        array = array.reshape(1, rows, width // HD, HD)
        return lax.all_to_all(array, "tm", split_axis=1, concat_axis=0, tiled=True)

    def to_frames(array):
        array = lax.all_to_all(array, "tm", split_axis=0, concat_axis=1, tiled=True)
        return array.reshape(rows, width)

    grads = temporal(*(to_patches(a) for a in (query, key_in, value, grad_out)))
    stacked = jnp.stack([to_frames(g) for g in grads])
    gathered = lax.all_gather(weights, "tm", axis=1, tiled=True)
    partial_sum = jnp.einsum("mic,mtc->it", gathered, stacked, preferred_element_type=F32)
    mine = lax.psum_scatter(partial_sum, "head", scatter_dimension=0, tiled=True)
    return mine.astype(BF16)


def chunk_kernel(info, *refs):
    pieces, (w_own, w_other, keep, pass_on, give, xs, grads, sums, sem) = refs[:5], refs[5:]
    patches, width = pieces[0].shape[2], pieces[0].shape[3]
    features = w_own.shape[1]
    scale = 1.0 / HD**0.5
    log2_scale = scale * 1.4426950408889634
    rows = 8 * GROUP

    per_half = width // 2
    copies = [[], []]
    for half in range(2):
        cs = pl.ds(half * per_half, per_half)
        places = (
            xs.at[:, 0:2, :, cs],
            xs.at[:, 2:4, :, cs],
            xs.at[:, 4:6, :, cs],
            xs.at[0:2, 6:8, :, cs],
            xs.at[2:4, 6:8, :, cs],
        )
        for at, (piece, place) in enumerate(zip(pieces, places)):
            copies[half].append(pltpu.make_async_copy(piece.at[:, :, :, cs], place, sem.at[half, at]))
    for copy in copies[0] + copies[1]:
        copy.start()

    r = lax.broadcasted_iota(jnp.int32, (rows, rows), 0)
    c = lax.broadcasted_iota(jnp.int32, (rows, rows), 1)
    bias = jnp.where((r % GROUP) == (c % GROUP), 0.0, -1e30).astype(F32)
    last = (((1,), (1,)), ((), ()))
    first = (((0,), (0,)), ((), ()))

    def attention(every):
        for start in range(0, len(every), UNITS):
            units = [(pl.ds(g * GROUP, GROUP), pl.ds(h * HD, HD)) for g, h in every[start : start + UNITS]]
            q, k, v, g = ([xs[which, :, ps, cs].reshape(rows, HD) for ps, cs in units] for which in range(4))
            scores = [lax.dot_general(b, a, last, preferred_element_type=F32) + bias for a, b in zip(q, k)]
            grad_probs = [lax.dot_general(b, a, last, preferred_element_type=F32) for a, b in zip(g, v)]
            probs_b, grad_scores = [], []
            for s, gp in zip(scores, grad_probs):
                e = jnp.exp2((s - jnp.max(s, axis=0, keepdims=True)) * log2_scale)
                p = e * (1.0 / jnp.sum(e, axis=0, keepdims=True))
                pb = p.astype(BF16)
                delta = jnp.sum(pb.astype(F32) * gp, axis=0, keepdims=True)
                probs_b.append(pb)
                grad_scores.append((p * (gp - delta)).astype(BF16))
            for at, (ps, cs) in enumerate(units):
                gs, pb = grad_scores[at], probs_b[at]
                gq = lax.dot_general(gs, k[at], first, preferred_element_type=F32) * scale
                gk = jnp.dot(gs, q[at], preferred_element_type=F32) * scale
                gv = jnp.dot(pb, g[at], preferred_element_type=F32)
                for m, grad in enumerate((gq, gk, gv)):
                    grads[m, :, ps, cs] = grad.astype(BF16).reshape(8, GROUP, HD)

    heads = per_half // HD
    for half in range(2):
        for copy in copies[half]:
            copy.wait()
        attention([(g, half * heads + h) for h in range(heads) for g in range(patches // GROUP)])

    for which, ws in enumerate((w_own, w_other)):
        base = (info[4] if which == 0 else 1 - info[4]) * features
        for start in range(0, features, TILE):
            total = None
            for m in range(3):
                flat = grads[m].reshape(8 * patches, width)
                term = lax.dot_general(flat, ws[m, start : start + TILE, :], last, preferred_element_type=F32)
                total = term if total is None else total + term
            sums[:, pl.ds(pl.multiple_of(base + start, TILE), TILE)] = total.astype(BF16)
    part = 2 * patches
    for x in range(4):
        out, row = ((keep, 0), (pass_on, 0), (give, 0), (give, part))[x]
        out[row : row + part, :] = sums[pl.ds(pl.multiple_of(info[x] * part, part), part), :]


def chunk(info, pieces, w_own, w_other):
    patches, width = pieces[0].shape[2], pieces[0].shape[3]
    features = w_own.shape[1]
    vmem = pl.BlockSpec(memory_space=pltpu.VMEM)
    return pl.pallas_call(
        chunk_kernel,
        in_specs=[pl.BlockSpec(memory_space=pltpu.SMEM)] + [pl.BlockSpec(memory_space=pl.ANY)] * 5 + [vmem] * 2,
        out_specs=[vmem] * 3,
        out_shape=[jax.ShapeDtypeStruct((n * patches, 2 * features), BF16) for n in (2, 2, 4)],
        scratch_shapes=[
            pltpu.VMEM((4, 8, patches, width), BF16),
            pltpu.VMEM((3, 8, patches, width), BF16),
            pltpu.VMEM((8 * patches, 2 * features), BF16),
            pltpu.SemaphoreType.DMA((2, 5)),
        ],
        compiler_params=pltpu.CompilerParams(vmem_limit_bytes=VMEM_MIB * 1024 * 1024),
        cost_estimate=pl.CostEstimate(
            flops=WEIGHT * (96 * patches * width * features + 80 * patches * 8 * GROUP * width),
            bytes_accessed=WEIGHT * (12 * features * width + 112 * patches * width),
            transcendentals=WEIGHT * (8 * patches * 8 * GROUP * width // HD),
        ),
        name="attention_and_product",
    )(info, *pieces, w_own, w_other)


def lay_kernel(core, early, final, crossed, out, kept_buffer, crossed_buffer, turned, sem):
    half, size = crossed.shape[0], early.shape[1]
    copies = [
        pltpu.make_async_copy(early.at[0], kept_buffer.at[0:size], sem.at[0]),
        pltpu.make_async_copy(final.at[0 : half - size], kept_buffer.at[size:half], sem.at[1]),
        pltpu.make_async_copy(crossed, crossed_buffer, sem.at[2]),
    ]
    for copy in copies:
        copy.start()
    copies[0].wait()
    copies[1].wait()
    writes = []
    for side, buffer in enumerate((kept_buffer, crossed_buffer)):
        if side == 1:
            copies[2].wait()
        turned[side] = buffer[...].T
        at = (core[0] if side == 0 else 1 - core[0]) * half
        place = out.at[:, pl.ds(pl.multiple_of(at, half), half)]
        writes.append(pltpu.make_async_copy(turned.at[side], place, sem.at[3 + side]))
        writes[-1].start()
    for write in writes:
        write.wait()


def lay_out(core, early, final, crossed):
    half, features = crossed.shape
    return pl.pallas_call(
        lay_kernel,
        in_specs=[pl.BlockSpec(memory_space=pltpu.SMEM)] + [pl.BlockSpec(memory_space=pl.ANY)] * 3,
        out_specs=pl.BlockSpec(memory_space=pl.ANY),
        out_shape=jax.ShapeDtypeStruct((features, 2 * half), BF16),
        scratch_shapes=[
            pltpu.VMEM((half, features), BF16),
            pltpu.VMEM((half, features), BF16),
            pltpu.VMEM((2, features, half), BF16),
            pltpu.SemaphoreType.DMA((5,)),
        ],
        compiler_params=pltpu.CompilerParams(vmem_limit_bytes=60 * 1024 * 1024),
        name="lay_out",
    )(core, early, final, crossed)


def swap(array, bit, n):
    return lax.ppermute(array, "tm", [(i, i ^ bit) for i in range(n)])


def after(array, *others):
    return lax.optimization_barrier((array, *others))[0]


COLUMN = ((0, 1, 2, 3), (2, 3, 0, 1), (3, 2, 1, 0), (1, 0, 3, 2))


def planes(query, key_in, value, grad_out, weights, *, n, m):
    rows, width = query.shape
    half = rows // 2
    chip, core = lax.axis_index("tm") // 2, lax.axis_index("tm") % 2
    plane = lax.axis_index("head")
    table = [[[COLUMN[r][z ^ x] ^ r for x in (0, 2, 1, 3)] for z in range(m)] for r in range(n // 2)]
    info = jnp.append(jnp.asarray(table, jnp.int32)[chip, plane], core)

    def together(*arrays):
        return lax.optimization_barrier(arrays)

    sizes = SIZES
    count = len(sizes)

    def rows_of(which, start, stop):
        arrays = (query, key_in, value, grad_out)
        return jnp.stack([lax.dynamic_slice_in_dim(a, which * half + start, stop - start, 0) for a in arrays])

    def meet(start, stop, *gate):
        theirs = swap(together(rows_of(1 - core, start, stop), *gate)[0], 1, n)
        return jnp.stack([rows_of(core, start, stop), theirs], axis=1), theirs

    begin, theirs = meet(0, sizes[0])
    rest, _ = meet(sizes[0], half, theirs)
    other = swap(after(weights, theirs), 1, n)
    own = [begin] + [
        lax.slice_in_dim(rest, sum(sizes[1:i]), sum(sizes[1 : i + 1]), axis=2) for i in range(1, count)
    ]

    def move(array, to):
        pairs = [(t * m + z, to(t // 2, t % 2, z)) for t in range(n) for z in range(m)]
        return lax.ppermute(array, ("tm", "head"), pairs)

    def in_plane(array):
        return move(array, lambda r, c, z: (COLUMN[r][z] * 2 + c) * m + z)

    def along_column(array):
        source = {(COLUMN[r][z], z): r for r in range(n // 2) for z in range(m)}
        return move(array, lambda s, c, z: (s * 2 + c) * m + source[s, z])

    def at_once(array, bit):
        return move(array, lambda r, c, z: (COLUMN[r][z] * 2 + (c ^ bit)) * m + r)

    def give_to(array, bit):
        return lax.ppermute(array, "head", [(z, z ^ bit) for z in range(m)])

    def add(a, b):
        return (a.astype(F32) + b.astype(F32)).astype(BF16)

    kernel, sums, moved = {}, {}, {}

    def first_add(k, got):
        keep, pass_on, _ = kernel[k]
        quarter = 2 * sizes[k]
        return add(keep, got[:quarter]), add(pass_on, got[quarter:])

    x1, x2 = swap(own[0], 2, n), swap(own[0], 4, n)
    low = high = None
    for k in range(count):
        gate = [kernel[k - 1][0]] if k >= 1 else []
        if k >= 2:
            sums[k - 2] = add(lows, give_to(highs, 2))
            gate += [sums[k - 2]]
        g1, g2 = together(x1, x2, *gate)[:2]
        g1, g2 = g1[:2], g2[2:]
        last = k == count - 1
        if not last:
            following = together(own[k + 1], g1, g2)[0]
            n1, n2 = swap(following, 2, n), swap(following, 4, n)
        pieces = (own[k], x1, x2, swap(g1, 4, n), swap(g2, 2, n))
        gate = []
        if k >= 1 and not last:
            lows, highs = first_add(k - 1, got)
            gate += [highs]
        pieces = together(*pieces, *gate)[:5]
        kernel[k] = chunk(info, pieces, weights, other)
        if last:
            lows, highs = first_add(k - 1, together(got, kernel[k][0])[0])
        got = give_to(kernel[k][2], 1)
        if not last:
            x1, x2 = n1, n2

    k = count - 1
    moved[0] = in_plane(together(sums[0], kernel[k][0], highs)[0])
    got2 = give_to(highs, 2)
    low, high = first_add(k, together(got, highs)[0])
    sums[k - 1] = add(lows, together(got2, high)[0])
    moved[k - 1] = in_plane(sums[k - 1])
    sums[k] = add(low, give_to(high, 2))
    early = jnp.concatenate([moved[at].reshape(2, sizes[at], -1) for at in range(k)], axis=1)
    early, final = together(along_column(together(early, sums[k])[0]), at_once(sums[k], 0))
    crossed = swap(jnp.concatenate([early[1], final[sizes[k] :]], axis=0), 1, n)
    return lay_out(core.reshape(1), early, final, crossed)


def solution(mesh):
    n, m = mesh.shape["tm"], mesh.shape["head"]
    per_device = functools.partial(planes, n=n, m=m) if n == 8 and m == 4 else any_mesh
    tokens = P("tm", "head")
    return jax.shard_map(
        per_device,
        mesh=mesh,
        in_specs=(tokens, tokens, tokens, tokens, P(None, "tm", "head")),
        out_specs=P("head", "tm"),
        check_vma=False,
    )
```
